128 devices in a mesh: dev: 128 (over y, z, x, core).
Axes of the slice: x: 4, y: 4, z: 4, core: 2. Of those that a mesh axis runs over, the one named last changes fastest.
Arguments:
- params: float32 [59, 524288], P(None, 'dev'), may hold values from -6.5 to 3
- first_moment: float32 [59, 524288], P(None, 'dev'), may hold values from -3 to 3
- second_moment: float32 [59, 524288], P(None, 'dev'), may hold values from 0.01 to 1
- send_table: int32 [128, 128, 64], P('dev'), may hold values from 0 to 4095
- tile_lists: int32 [8192, 128], P('dev'), may hold values from 0 to 8191, as said below
- list_length: int32 [8192], P('dev'), may hold values from 42 to 128, as said below
- target: float32 [3, 8192, 256], P(None, 'dev'), may hold values from 0.05 to 1
Outputs:
- new_params: float32 [59, 524288], P(None, 'dev')
- new_first: float32 [59, 524288], P(None, 'dev')
- new_second: float32 [59, 524288], P(None, 'dev')
- mean_loss: float32 [], replicated
The draws below stay inside these ranges and needn't reach their ends.
Inputs may be any that keep to these rules, and one draw needn't show every extreme that they name: `tile_lists`: every entry names a slot of its tile's view: sender * 64 + view * 16 + k. `list_length`: some tile of every device has a full list.
All inputs are finite; a program needn't handle non-finite values.
Results may differ from the reference program's by a relative error of at most 0.0017.
Values may be sent and summed in bfloat16 or wider, within the bound.
No kernel may reach another device: no remote copies, remote signals or barrier semaphores. Data moves between devices by JAX's collectives and lax.ppermute only.
A program may use at most 128 MiB of HBM per device.

```python
import math
import jax
import jax.numpy as jnp
from jax import lax

PARAMS = 59
VIEWS = 4
G_DEV = 4096
TILES_DEV = 64
LIST_MAX = 128
CAPV = 16
CAP = 64
G_ALL = 524288
TILES_ALL = 8192
N_DEV = 128


def routing(key):
    subkeys = jax.random.split(jax.random.fold_in(key, 7), 5)
    counts = jax.random.randint(subkeys[0], (N_DEV, N_DEV, VIEWS), 1, CAPV + 1)
    receiver = jnp.arange(N_DEV)[:, None]
    view_index = jnp.arange(VIEWS)[None, :]
    forced = (receiver * 5 + view_index * 3 + 1) % N_DEV
    counts = counts.at[receiver, forced, view_index].set(CAPV)
    send_table = jax.random.randint(subkeys[1], (N_DEV, N_DEV, CAP), 0, G_DEV)
    tile_view = jnp.arange(TILES_DEV) // (TILES_DEV // VIEWS)
    sender_pick = jax.random.randint(subkeys[2], (N_DEV, TILES_DEV, LIST_MAX), 0, N_DEV)
    live_count = counts[jnp.arange(N_DEV)[:, None, None], sender_pick, tile_view[None, :, None]]
    within = jax.random.randint(subkeys[3], (N_DEV, TILES_DEV, LIST_MAX), 0, 1048576) % live_count
    tile_lists = sender_pick * CAP + tile_view[None, :, None] * CAPV + within
    lengths = jax.random.randint(subkeys[4], (N_DEV, TILES_DEV), LIST_MAX // 3, LIST_MAX + 1)
    full_tile = jnp.arange(N_DEV) * 3 % TILES_DEV
    lengths = lengths.at[jnp.arange(N_DEV), full_tile].set(LIST_MAX)
    return (send_table.astype(jnp.int32), tile_lists.reshape(TILES_ALL, LIST_MAX).astype(jnp.int32), lengths.reshape(TILES_ALL).astype(jnp.int32))


def draw_send_table(key, part):
    shared = routing(key)
    return shared[0]


def draw_tile_lists(key, part):
    shared = routing(key)
    return shared[1]


def draw_list_length(key, part):
    shared = routing(key)
    return shared[2]


def uniform_rows(key, count, low, high):
    return jax.random.uniform(key, (count, G_ALL), jnp.float32, low, high)


def draw_params(key, part):
    key = jax.random.fold_in(key, 1)
    subkeys = jax.random.split(key, 7)
    position = jnp.clip(0.7 * jax.random.normal(subkeys[0], (3, G_ALL), jnp.float32), -3.0, 3.0)
    log_extent = uniform_rows(subkeys[1], 3, -3.5, -2.2)
    quat_w = uniform_rows(subkeys[2], 1, 0.5, 1.5)
    quat_rest = uniform_rows(subkeys[3], 3, -1.0, 1.0)
    logit = uniform_rows(subkeys[4], 1, -5.5, -1.8)
    base_color = uniform_rows(subkeys[5], 3, 0.2, 1.2)
    higher = jnp.clip(0.15 * jax.random.normal(subkeys[6], (45, G_ALL), jnp.float32), -0.6, 0.6)
    return jnp.concatenate([position, log_extent, quat_w, quat_rest, logit, base_color, higher], axis=0)


def block_scale(stream_key, shape, pieces, smallest, largest):
    level = 1.0
    for dim, parts in pieces:
        heights = jax.random.uniform(jax.random.fold_in(jax.random.fold_in(stream_key, 6), dim), (parts,), jnp.float32, smallest / len(pieces), largest / len(pieces))
        level = level * jnp.repeat(jnp.exp(heights), shape[dim] // parts).reshape((-1,) + (1,) * (len(shape) - 1 - dim))
    return level


def scatter_about(own_key, shape, scale, bound, cuts=(), kind=jnp.bfloat16):
    gain = block_scale(own_key, shape, cuts, -0.22, 0.18) if cuts else 1.0
    array = jax.random.normal(own_key, shape, jnp.float32) * scale * gain
    return jnp.minimum(jnp.maximum(array, -bound), bound).astype(kind)


def setup_inputs(seed: int = 0) -> dict:
    key_of = jax.random.split(jax.random.key(seed), 8)
    return {
        "params": draw_params(jax.random.fold_in(key_of[7], 71), 0),
        "first_moment": scatter_about(key_of[1], (PARAMS, G_ALL), 0.5, 3.0, ((1, 128),), jnp.float32),
        "second_moment": jnp.clip(jnp.exp(math.log(1.0) - 4.6051702 * jax.random.uniform(key_of[2], (PARAMS, G_ALL), jnp.float32) ** block_scale(key_of[2], (PARAMS, G_ALL), ((1, 128),), -0.2, 0.2)), 0.01, 1.0),
        "send_table": draw_send_table(jax.random.fold_in(key_of[7], 71), 0),
        "tile_lists": draw_tile_lists(jax.random.fold_in(key_of[7], 71), 0),
        "list_length": draw_list_length(jax.random.fold_in(key_of[7], 71), 0),
        "target": jnp.clip(0.05 + 0.95 * jax.random.uniform(key_of[6], (3, TILES_ALL, 256), jnp.float32) ** block_scale(key_of[6], (3, TILES_ALL, 256), ((1, 128),), -0.2, 0.2), 0.05, 1.0),
    }


focal_length = 40.0
camera_pitch = 0.35
dilation = 0.3
window_sigma = 1.5
stabilizer_one = 0.0001
stabilizer_two = 0.0009
loss_blend = 0.2
beta_first = 0.9
beta_second = 0.999
adam_step = 100.0
learning_rate = 0.001
adam_epsilon = 1e-08
harmonic_zero = 0.28209479177387814
harmonic_one = 0.4886025119029199
harmonic_two = [1.0925484305920792, -1.0925484305920792, 0.31539156525252005, -1.0925484305920792, 0.5462742152960396]
harmonic_three = [-0.5900435899266435, 2.890611442640554, -0.4570457994644658, 0.3731763325901154, -0.4570457994644658, 1.445305721320277, -0.5900435899266435]

def harmonics(look_x, look_y, look_z):
    xx = look_x * look_x
    yy = look_y * look_y
    zz = look_z * look_z
    return [harmonic_zero + 0.0 * look_x, -harmonic_one * look_y, harmonic_one * look_z, -harmonic_one * look_x, harmonic_two[0] * look_x * look_y, harmonic_two[1] * look_y * look_z, harmonic_two[2] * (2.0 * zz - xx - yy), harmonic_two[3] * look_x * look_z, harmonic_two[4] * (xx - yy), harmonic_three[0] * look_y * (3.0 * xx - yy), harmonic_three[1] * look_x * look_y * look_z, harmonic_three[2] * look_y * (4.0 * zz - xx - yy), harmonic_three[3] * look_z * (2.0 * zz - 3.0 * xx - 3.0 * yy), harmonic_three[4] * look_x * (4.0 * zz - xx - yy), harmonic_three[5] * look_z * (xx - yy), harmonic_three[6] * look_x * (xx - 3.0 * yy)]

def project(columns, slot_view):
    yaw_angle = slot_view.astype(jnp.float32) * (2.0 * math.pi / VIEWS) + 0.3
    cosine_yaw = jnp.cos(yaw_angle)
    sine_yaw = jnp.sin(yaw_angle)
    sine_pitch = math.sin(camera_pitch)
    cosine_pitch = math.cos(camera_pitch)
    right_axis = (cosine_yaw, 0.0 * cosine_yaw, -sine_yaw)
    upward = (sine_pitch * sine_yaw, cosine_pitch + 0.0 * cosine_yaw, sine_pitch * cosine_yaw)
    look_axis = (cosine_pitch * sine_yaw, -sine_pitch + 0.0 * cosine_yaw, cosine_pitch * cosine_yaw)
    position = columns[0:3]
    extent = jnp.exp(columns[3:6])
    quaternion = columns[6:10] / jnp.sqrt(lax.optimization_barrier(jnp.sum(columns[6:10] * columns[6:10], axis=0)))
    quat_w, quat_x, quat_y, quat_z = (quaternion[0], quaternion[1], quaternion[2], quaternion[3])
    rotation = [[1.0 - 2.0 * (quat_y * quat_y + quat_z * quat_z), 2.0 * (quat_x * quat_y - quat_w * quat_z), 2.0 * (quat_x * quat_z + quat_w * quat_y)], [2.0 * (quat_x * quat_y + quat_w * quat_z), 1.0 - 2.0 * (quat_x * quat_x + quat_z * quat_z), 2.0 * (quat_y * quat_z - quat_w * quat_x)], [2.0 * (quat_x * quat_z - quat_w * quat_y), 2.0 * (quat_y * quat_z + quat_w * quat_x), 1.0 - 2.0 * (quat_x * quat_x + quat_y * quat_y)]]
    along_right = [focal_length * extent[k] * sum((right_axis[i] * rotation[i][k] for i in range(3))) for k in range(3)]
    along_up = [focal_length * extent[k] * sum((upward[i] * rotation[i][k] for i in range(3))) for k in range(3)]
    spread_xx = sum((along_right[k] * along_right[k] for k in range(3))) + dilation
    spread_xy = sum((along_right[k] * along_up[k] for k in range(3)))
    spread_yy = sum((along_up[k] * along_up[k] for k in range(3))) + dilation
    determinant = spread_xx * spread_yy - spread_xy * spread_xy
    center_x = 8.0 + 6.0 * jnp.tanh(sum((right_axis[i] * position[i] for i in range(3))))
    center_y = 8.0 + 6.0 * jnp.tanh(sum((upward[i] * position[i] for i in range(3))))
    opacity = jax.nn.sigmoid(columns[10])
    basis = harmonics(look_axis[0], look_axis[1], look_axis[2])
    colors = [0.5 + sum((basis[k] * columns[11 + 3 * k + channel] for k in range(16))) for channel in range(3)]
    return jnp.stack([center_x, center_y, spread_yy / determinant, -spread_xy / determinant, spread_xx / determinant, opacity] + colors, axis=0)

def round_through(values):
    rounded = lax.optimization_barrier(values.astype(jnp.bfloat16)).astype(jnp.float32)
    return values + lax.stop_gradient(rounded - values)

def window_table():
    offsets = jnp.arange(11).astype(jnp.float32) - 5.0
    normalizer = jnp.sum(jnp.exp(-offsets * offsets / (2.0 * window_sigma * window_sigma)))
    places = jnp.arange(16)
    distance = (places[:, None] - places[None, :]).astype(jnp.float32)
    table = jnp.exp(-distance * distance / (2.0 * window_sigma * window_sigma)) / normalizer
    return jnp.where(jnp.abs(distance) <= 5.0, table, 0.0)

def window_mean(field, table):
    return jnp.einsum('ij,cbjk,lk->cbil', table, field, table, precision=lax.Precision.HIGHEST)

def tile_loss(row_values, tile_list, tile_length, tile_target):
    entries = row_values[:, tile_list]
    count = tile_list.shape[1]
    live_mask = (jnp.arange(count)[None, :] < tile_length[:, None]).astype(jnp.float32)
    pixel = jnp.arange(256)
    pixel_x = (pixel % 16).astype(jnp.float32) + 0.5
    pixel_y = (pixel // 16).astype(jnp.float32) + 0.5
    offset_x = pixel_x[None, :, None] - entries[0][:, None, :]
    offset_y = pixel_y[None, :, None] - entries[1][:, None, :]
    exponent = -0.5 * (entries[2][:, None, :] * offset_x * offset_x + entries[4][:, None, :] * offset_y * offset_y) - entries[3][:, None, :] * offset_x * offset_y
    coverage = entries[5][:, None, :] * jnp.exp(exponent) * live_mask[:, None, :]
    log_clear = jnp.log1p(-coverage)
    accrued = jnp.cumsum(log_clear, axis=-1) - log_clear
    weight = jnp.exp(accrued) * coverage
    rendered = jnp.einsum('btl,cbl->cbt', weight, entries[6:9], precision=lax.Precision.HIGHEST)
    blocks = tile_list.shape[0]
    image_x = rendered.reshape(3, blocks, 16, 16)
    image_y = tile_target.reshape(3, blocks, 16, 16)
    table = window_table()
    mean_x = window_mean(image_x, table)
    mean_y = window_mean(image_y, table)
    var_x = window_mean(image_x * image_x, table) - mean_x * mean_x
    var_y = window_mean(image_y * image_y, table) - mean_y * mean_y
    covariance = window_mean(image_x * image_y, table) - mean_x * mean_y
    similarity = (2.0 * mean_x * mean_y + stabilizer_one) * (2.0 * covariance + stabilizer_two) / ((mean_x * mean_x + mean_y * mean_y + stabilizer_one) * (var_x + var_y + stabilizer_two))
    pixel_loss = (1.0 - loss_blend) * jnp.abs(image_x - image_y) + loss_blend * (1.0 - similarity)
    return jnp.sum(pixel_loss)

def reference(params, first_moment, second_moment, send_table, tile_lists, list_length, target):
    sender = jnp.arange(N_DEV, dtype=jnp.int32)[:, None, None]
    global_index = (sender * G_DEV + send_table).transpose(1, 0, 2).reshape(N_DEV, N_DEV * CAP)
    position = jnp.arange(N_DEV * CAP, dtype=jnp.int32)
    slot_view = position % CAP // CAPV
    lists = tile_lists.reshape(N_DEV, TILES_DEV, LIST_MAX)
    lengths = list_length.reshape(N_DEV, TILES_DEV)
    targets = jnp.moveaxis(target.reshape(3, N_DEV, TILES_DEV, 256), 1, 0)

    def per_device(inputs):
        gaussian_slot, tile_list, tile_length, tile_target = inputs
        columns = params[:, gaussian_slot]

        def render_loss(values):
            return tile_loss(round_through(project(values, slot_view)), tile_list, tile_length, tile_target)
        return jax.value_and_grad(render_loss)(columns)
    device_losses, column_grads = lax.map(per_device, (global_index, lists, lengths, targets))
    flat_grads = jnp.moveaxis(column_grads, 0, 1).reshape(PARAMS, N_DEV * N_DEV * CAP)
    gradient = jnp.zeros_like(params).at[:, global_index.reshape(-1)].add(flat_grads)
    mean_loss = jnp.sum(device_losses) / (3.0 * TILES_ALL * 256)
    new_first = beta_first * first_moment + (1.0 - beta_first) * gradient
    new_second = beta_second * second_moment + (1.0 - beta_second) * gradient * gradient
    corrected_first = new_first / (1.0 - beta_first ** adam_step)
    corrected_second = new_second / (1.0 - beta_second ** adam_step)
    new_params = params - learning_rate * corrected_first / (jnp.sqrt(corrected_second) + adam_epsilon)
    return (new_params, new_first, new_second, mean_loss)
```

```python
import functools
import math

import jax
import jax.numpy as jnp
import numpy as np
from jax import lax
from jax.experimental import pallas as pl
from jax.experimental.pallas import tpu as pltpu
from jax.sharding import PartitionSpec as P

VIEWS = 4
CAPV = 16
ROWS = 9
PAYLOAD = 640

focal_length = 40.0
camera_pitch = 0.35
dilation = 0.3
window_sigma = 1.5
stabilizer_one = 0.0001
stabilizer_two = 0.0009
loss_blend = 0.2
beta_first = 0.9
beta_second = 0.999
adam_step = 100.0
learning_rate = 0.001
adam_epsilon = 1e-08
log2e = math.log2(math.e)
harmonic_zero = 0.28209479177387814
harmonic_one = 0.4886025119029199
harmonic_two = [
    1.0925484305920792,
    -1.0925484305920792,
    0.31539156525252005,
    -1.0925484305920792,
    0.5462742152960396,
]
harmonic_three = [
    -0.5900435899266435,
    2.890611442640554,
    -0.4570457994644658,
    0.3731763325901154,
    -0.4570457994644658,
    1.445305721320277,
    -0.5900435899266435,
]
f32 = jnp.float32
bf16 = jnp.bfloat16
i32 = jnp.int32
HIGHEST = lax.Precision.HIGHEST


def harmonics(look_x, look_y, look_z):
    xx = look_x * look_x
    yy = look_y * look_y
    zz = look_z * look_z
    return [
        harmonic_zero,
        -harmonic_one * look_y,
        harmonic_one * look_z,
        -harmonic_one * look_x,
        harmonic_two[0] * look_x * look_y,
        harmonic_two[1] * look_y * look_z,
        harmonic_two[2] * (2.0 * zz - xx - yy),
        harmonic_two[3] * look_x * look_z,
        harmonic_two[4] * (xx - yy),
        harmonic_three[0] * look_y * (3.0 * xx - yy),
        harmonic_three[1] * look_x * look_y * look_z,
        harmonic_three[2] * look_y * (4.0 * zz - xx - yy),
        harmonic_three[3] * look_z * (2.0 * zz - 3.0 * xx - 3.0 * yy),
        harmonic_three[4] * look_x * (4.0 * zz - xx - yy),
        harmonic_three[5] * look_z * (xx - yy),
        harmonic_three[6] * look_x * (xx - 3.0 * yy),
    ]


def camera(view):
    yaw = 2.0 * math.pi * view / VIEWS + 0.3
    cy, sy = math.cos(yaw), math.sin(yaw)
    cp, sp = math.cos(camera_pitch), math.sin(camera_pitch)
    return (cy, 0.0, -sy), (sp * sy, cp, sp * cy), (cp * sy, -sp, cp * cy)


def basis_table():
    table = np.zeros((16, 59), np.float64)
    for view in range(VIEWS):
        basis = harmonics(*camera(view)[2])
        for k in range(16):
            for channel in range(3):
                table[3 * view + channel, 11 + 3 * k + channel] = basis[k]
    return table


def spread_table():
    table = np.zeros((64, 32), np.float64)
    table[:59, :16] = basis_table().T
    for row in range(11):
        table[row, 16 + row] = 1.0
    return table.astype(np.float32)


def window_matrix():
    offsets = np.arange(11) - 5.0
    normalizer = np.sum(np.exp(-offsets * offsets / (2.0 * window_sigma**2)))
    distance = np.arange(16)[:, None] - np.arange(16)[None, :]
    table = np.exp(-distance * distance / (2.0 * window_sigma**2)) / normalizer
    table = np.where(np.abs(distance) <= 5, table, 0.0)
    return np.kron(table, table).astype(np.float32)


def dot(table, axis):
    total = None
    for entry, weight in zip(table, axis):
        if weight != 0.0:
            total = entry * weight if total is None else total + entry * weight
    return total


def geometry(rows):
    extent = [jnp.exp(rows[3 + k]) for k in range(3)]
    norm = jnp.sqrt(
        rows[6] * rows[6] + rows[7] * rows[7] + rows[8] * rows[8] + rows[9] * rows[9]
    )
    w, x, y, z = (rows[6 + i] / norm for i in range(4))
    rotation = [
        [1.0 - 2.0 * (y * y + z * z), 2.0 * (x * y - w * z), 2.0 * (x * z + w * y)],
        [2.0 * (x * y + w * z), 1.0 - 2.0 * (x * x + z * z), 2.0 * (y * z - w * x)],
        [2.0 * (x * z - w * y), 2.0 * (y * z + w * x), 1.0 - 2.0 * (x * x + y * y)],
    ]
    scaled = [[focal_length * extent[k] * rotation[i][k] for k in range(3)] for i in range(3)]
    return extent, norm, (w, x, y, z), scaled


def view_geometry(rows, scaled, view):
    right, upward, _ = camera(view)
    tanh_x = jnp.tanh(dot(rows[0:3], right))
    tanh_y = jnp.tanh(dot(rows[0:3], upward))
    along_right = [dot([scaled[i][k] for i in range(3)], right) for k in range(3)]
    along_up = [dot([scaled[i][k] for i in range(3)], upward) for k in range(3)]
    spread_xx = sum(along_right[k] * along_right[k] for k in range(3)) + dilation
    spread_xy = sum(along_right[k] * along_up[k] for k in range(3))
    spread_yy = sum(along_up[k] * along_up[k] for k in range(3)) + dilation
    inverse = 1.0 / (spread_xx * spread_yy - spread_xy * spread_xy)
    conic = (spread_yy * inverse, -spread_xy * inverse, spread_xx * inverse)
    return tanh_x, tanh_y, along_right, along_up, conic


def iota(shape, dim, kind=i32):
    return lax.broadcasted_iota(i32, shape, dim).astype(kind)


def project_kernel(params_ref, table_ref, basis_ref, out_ref, rows_ref, packed_ref):
    lead = params_ref[0:16, :].reshape(16, 32, 128)
    rows = [lead[i] for i in range(11)]
    colors = jnp.dot(
        basis_ref[...], params_ref[...], precision=HIGHEST, preferred_element_type=f32
    )
    colors = 0.5 + colors.reshape(16, 32, 128)
    _, _, _, scaled = geometry(rows)
    opacity = 1.0 / (1.0 + jnp.exp(-rows[10]))
    for view in range(VIEWS):
        tanh_x, tanh_y, _, _, conic = view_geometry(rows, scaled, view)
        projected = [8.0 + 6.0 * tanh_x, 8.0 + 6.0 * tanh_y, *conic, opacity]
        projected += [colors[3 * view + channel] for channel in range(3)]
        for f in range(ROWS):
            rows_ref[view * ROWS + f] = projected[f].astype(bf16).astype(f32)

    slots = table_ref[...].T
    packed_ref[576:640, :] = jnp.zeros((64, 128), f32)
    for view in range(VIEWS):
        index = slots[view * CAPV : (view + 1) * CAPV, :]
        high = lax.shift_right_logical(index, 7)
        low = index & 127

        def step(h, found, view=view, high=high, low=low):
            here = high == h
            result = []
            for f in range(ROWS):
                row = rows_ref[view * ROWS + f, pl.ds(h, 1), :]
                row = jnp.broadcast_to(row, (CAPV, 128))
                taken = jnp.take_along_axis(row, low, axis=1, mode="promise_in_bounds")
                result.append(jnp.where(here, taken, found[f]))
            return result

        found = [jnp.zeros((CAPV, 128), f32)] * ROWS
        found = lax.fori_loop(0, 32, step, found, unroll=8)
        for f in range(ROWS):
            packed_ref[pl.ds(64 * f + view * CAPV, CAPV), :] = found[f]
    out_ref[:, 0, :] = packed_ref[...].T


def render_kernel(
    rows_ref,
    lists_ref,
    length_ref,
    target_ref,
    window_ref,
    out_ref,
    slots_ref,
    entry_ref,
    column_ref,
    cover_ref,
    weight_ref,
    image_ref,
    partial_ref,
    moment_ref,
    spread_ref,
    hot_ref,
    total_ref,
):
    lists = lists_ref[...]
    slot = lists & 63
    strays = jnp.where(lax.shift_right_logical(slot, 4) != iota((64, 128), 0) // 16, 1, 0)
    regular = jnp.max(strays) == 0

    slots_ref[...] = rows_ref[:, 0, :].T
    entry_ref[...] = jnp.zeros((ROWS, 64, 128), f32)
    for view in range(VIEWS):
        first = jnp.where(regular, view, 0)
        last = jnp.where(regular, view + 1, VIEWS)

        def block(b, carry, view=view):
            at = pl.ds(pl.multiple_of(b * 16, 16), 16)
            here = lists_ref[at, :]
            sender = lax.shift_right_logical(here, 6)
            place = here & 63
            found = [entry_ref[f, at, :] for f in range(ROWS)]
            for k in range(CAPV):
                hit = place == view * CAPV + k
                for f in range(ROWS):
                    row = slots_ref[64 * f + view * CAPV + k : 64 * f + view * CAPV + k + 1, :]
                    row = jnp.broadcast_to(row, (16, 128))
                    taken = jnp.take_along_axis(row, sender, axis=1, mode="promise_in_bounds")
                    found[f] = jnp.where(hit, taken, found[f])
            for f in range(ROWS):
                entry_ref[f, at, :] = found[f]
            return carry

        lax.fori_loop(first, last, block, 0)

    length = jnp.concatenate([length_ref[...], length_ref[...]], axis=1)
    live = iota((128, 128), 0) < length
    for f in range(ROWS):
        both = jnp.concatenate([entry_ref[f], entry_ref[f]], axis=0).T
        column_ref[f] = both
        if f == 5:
            column_ref[ROWS] = jnp.where(live, both, 0.0)

    lane = iota((8, 128), 1)
    base_y = jnp.where(lane < 64, 0.5, 8.5)

    def entry_row(f, j):
        return jnp.broadcast_to(column_ref[f, pl.ds(j, 1), :], (8, 128))

    for half in range(2):
        place_x = iota((8, 128), 0, f32) + (8.0 * half + 0.5)

        def forward(j, carry, half=half, place_x=place_x):
            clear, image = carry
            clear, image = list(clear), [list(c) for c in image]
            dx = place_x - entry_row(0, j)
            dy = base_y - entry_row(1, j)
            conic0 = entry_row(2, j) * (-0.5 * log2e)
            conic1 = entry_row(3, j) * (-log2e)
            conic2 = entry_row(4, j) * (-0.5 * log2e)
            opacity = entry_row(ROWS, j)
            color = [entry_row(6 + c, j) for c in range(3)]
            cross = conic1 * dx
            exponent = conic0 * dx * dx + dy * (cross + conic2 * dy)
            slope = cross + conic2 * (2.0 * dy + 1.0)
            bend = 2.0 * conic2
            for y in range(8):
                coverage = opacity * jnp.exp2(exponent)
                weight = clear[y] * coverage
                clear[y] = clear[y] - weight
                for c in range(3):
                    image[c][y] = image[c][y] + weight * color[c]
                cover_ref[j, 2 * y + half] = coverage
                weight_ref[j, 2 * y + half] = weight
                if y < 7:
                    exponent = exponent + slope
                    slope = slope + bend
            return clear, image

        zero = jnp.zeros((8, 128), f32)
        start = ([jnp.ones((8, 128), f32)] * 8, [[zero] * 8] * 3)
        _, image = lax.fori_loop(0, 128, forward, start, unroll=2)
        for c in range(3):
            for y in range(8):
                image_ref[c, 16 * y + 8 * half : 16 * y + 8 * half + 8, :] = image[c][y]

    left = iota((128, 128), 1) < 64
    zeros = jnp.zeros((128, 128), f32)

    def swap(block):
        return pltpu.roll(block, 64, 1)

    image = [image_ref[c] for c in range(3)]
    top = jnp.concatenate(
        [jnp.where(left, image[0], swap(image[1])), jnp.where(left, image[2], zeros)], axis=1
    )
    bottom = jnp.concatenate(
        [jnp.where(left, swap(image[0]), image[1]), jnp.where(left, swap(image[2]), zeros)],
        axis=1,
    )
    shown = jnp.concatenate([top, bottom], axis=0)
    goal = jnp.concatenate(
        [target_ref[0], target_ref[1], target_ref[2], jnp.zeros((64, 256), f32)], axis=0
    ).T

    def window_mean(field):
        return jnp.dot(
            window_ref[...], field, precision=HIGHEST, preferred_element_type=f32
        )

    mean_x = window_mean(shown)
    mean_y = window_mean(goal)
    var_x = window_mean(shown * shown) - mean_x * mean_x
    var_y = window_mean(goal * goal) - mean_y * mean_y
    covariance = window_mean(shown * goal) - mean_x * mean_y
    top_one = 2.0 * mean_x * mean_y + stabilizer_one
    top_two = 2.0 * covariance + stabilizer_two
    under_one = 1.0 / (mean_x * mean_x + mean_y * mean_y + stabilizer_one)
    under_two = 1.0 / (var_x + var_y + stabilizer_two)
    under = under_one * under_two
    similarity = top_one * top_two * under
    difference = shown - goal
    pixel_loss = (1.0 - loss_blend) * jnp.abs(difference) + loss_blend * (1.0 - similarity)
    used = iota((256, 256), 1) < 192
    loss = jnp.sum(jnp.where(used, pixel_loss, 0.0))
    by_product = 2.0 * top_one * under
    by_square = -similarity * under_two
    by_mean = (
        2.0 * mean_y * top_two * under
        - 2.0 * mean_x * similarity * under_one
        - mean_y * by_product
        - 2.0 * mean_x * by_square
    )
    slope = (1.0 - loss_blend) * jnp.where(
        difference > 0.0, 1.0, jnp.where(difference < 0.0, -1.0, 0.0)
    ) - loss_blend * (
        window_mean(by_mean)
        + 2.0 * shown * window_mean(by_square)
        + goal * window_mean(by_product)
    )
    top, bottom = slope[0:128, 0:128], slope[128:256, 0:128]
    image_ref[0] = jnp.where(left, top, swap(bottom))
    image_ref[1] = jnp.where(left, swap(top), bottom)
    top, bottom = slope[0:128, 128:256], slope[128:256, 128:256]
    image_ref[2] = jnp.where(left, top, swap(bottom))

    for half in range(2):
        place_x = iota((8, 128), 0, f32) + (8.0 * half - 7.5)
        slope = [
            [image_ref[c, 16 * y + 8 * half : 16 * y + 8 * half + 8, :] for y in range(8)]
            for c in range(3)
        ]

        def backward(i, behind, half=half, place_x=place_x, slope=slope):
            j = 127 - i
            behind = list(behind)
            color = [entry_row(6 + c, j) for c in range(3)]
            by_color = [None] * 3
            sum0 = sum1 = sum2 = None
            for y in range(7, -1, -1):
                coverage = cover_ref[j, 2 * y + half]
                weight = weight_ref[j, 2 * y + half]
                own = slope[0][y] * color[0] + slope[1][y] * color[1] + slope[2][y] * color[2]
                excess = own - behind[y]
                behind[y] = behind[y] + coverage * excess
                push = weight * excess
                for c in range(3):
                    term = weight * slope[c][y]
                    by_color[c] = term if by_color[c] is None else by_color[c] + term
                sum0 = push if sum0 is None else sum0 + push
                if y > 0:
                    sum1 = sum0 if sum1 is None else sum1 + sum0
                    sum2 = sum1 if sum2 is None else sum2 + sum1
            along = sum0 * place_x
            parts = [sum0, along, along * place_x, sum1, sum1 * place_x, sum2, *by_color]
            if half == 0:
                for n in range(ROWS):
                    partial_ref[n, j] = parts[n]
            else:
                for n in range(ROWS):
                    whole = jnp.sum(parts[n] + partial_ref[n, j], axis=0, keepdims=True)
                    moment_ref[n, pl.ds(j, 1), :] = whole
            return behind

        lax.fori_loop(0, 128, backward, [jnp.zeros((8, 128), f32)] * 8, unroll=2)

    at_x = 8.0 - column_ref[0]
    at_y = jnp.where(left, 0.5, 8.5) - column_ref[1]
    m, mx, mxx = moment_ref[0], moment_ref[1], moment_ref[2]
    my, mxy = moment_ref[3], moment_ref[4]
    myy = 2.0 * moment_ref[5] - my
    about_x = mx + at_x * m
    about_y = my + at_y * m
    about_xx = mxx + at_x * (mx + about_x)
    about_yy = myy + at_y * (my + about_y)
    about_xy = mxy + at_y * mx + at_x * about_y
    conic0, conic1, conic2 = column_ref[2], column_ref[3], column_ref[4]
    grads = [
        conic0 * about_x + conic1 * about_y,
        conic2 * about_y + conic1 * about_x,
        -0.5 * about_xx,
        -about_xy,
        -0.5 * about_yy,
        m / column_ref[5],
        moment_ref[6],
        moment_ref[7],
        moment_ref[8],
    ]
    for f in range(ROWS):
        both = grads[f].T
        whole = both[0:64] + both[64:128]
        coarse = whole.astype(bf16).astype(f32)
        entry_ref[f] = coarse
        moment_ref[f, 0:64, :] = whole - coarse

    which8 = iota((8, 128), 0)
    which256 = iota((256, 128), 0)
    nothing = jnp.zeros((8, 128), f32)
    for view in range(VIEWS):
        first = jnp.where(regular, view, 0)
        last = jnp.where(regular, view + 1, VIEWS)
        total_ref[...] = jnp.zeros((160, 256), f32)

        def block(b, carry, view=view):
            for t in range(16):
                tile = b * 16 + t
                here = lists_ref[pl.ds(tile, 1), :]
                pair = lax.shift_right_logical(here & 63, 1)
                hit = jnp.broadcast_to(pair, (8, 128)) == which8 + view * 8
                lanes = slice(128 * t, 128 * t + 128)
                for part, source in enumerate((entry_ref, moment_ref)):
                    pieces = []
                    for f in range(ROWS):
                        row = jnp.broadcast_to(source[f, pl.ds(tile, 1), :], (8, 128))
                        pieces.append(jnp.where(hit, row, 0.0))
                    pieces.append(nothing)
                    spread_ref[80 * part : 80 * part + 80, lanes] = jnp.concatenate(
                        pieces, axis=0
                    ).astype(bf16)
                key = (here & 1) * 128 + lax.shift_right_logical(here, 6)
                hot = jnp.broadcast_to(key, (256, 128)) == which256
                hot_ref[:, lanes] = jnp.where(hot, 1.0, 0.0).astype(bf16)
            total_ref[...] += lax.dot_general(
                spread_ref[...],
                hot_ref[...],
                (((1,), (1,)), ((), ())),
                preferred_element_type=f32,
            )
            return carry

        lax.fori_loop(first, last, block, 0)
        total = total_ref[0:80, :] + total_ref[80:160, :]
        for parity in range(2):
            at = 160 * view + 80 * parity
            slots_ref[at : at + 72, :] = total[0:72, 128 * parity : 128 * parity + 128]
            slots_ref[at + 72 : at + 80, :] = jnp.full((8, 128), loss, f32)
    out_ref[:, 0, :] = slots_ref[...].T


def update_kernel(
    pixels,
    grads_ref,
    table_ref,
    spread_table_ref,
    params_ref,
    first_ref,
    second_ref,
    new_params_ref,
    new_first_ref,
    new_second_ref,
    loss_ref,
    coarse_ref,
    fine_ref,
    high_ref,
    low_ref,
    spread_ref,
    hot_ref,
    stack_ref,
):
    packed = grads_ref[:, 0, :].T
    loss_ref[...] = jnp.sum(packed[72:73, :], axis=1, keepdims=True) * (1.0 / pixels)
    coarse = packed.astype(bf16).astype(f32)
    coarse_ref[...] = coarse
    fine_ref[...] = packed - coarse
    slots = table_ref[...].T
    high_ref[...] = lax.shift_right_logical(slots, 8)
    low_ref[...] = slots & 255

    lead = params_ref[0:16, :].reshape(16, 16, 256)
    rows = [lead[i] for i in range(11)]
    extent, norm, (w, x, y, z), scaled = geometry(rows)
    opacity = 1.0 / (1.0 + jnp.exp(-rows[10]))
    which16 = iota((16, 128), 0)
    which256 = iota((256, 128), 0)

    zero = jnp.zeros((16, 256), f32)
    by_position = [zero] * 3
    by_extent = [zero] * 3
    by_rotation = [[zero] * 3 for _ in range(3)]
    by_opacity = zero
    by_color = []
    for view in range(VIEWS):
        for k in range(CAPV):
            slot = view * CAPV + k
            lanes = slice(128 * k, 128 * k + 128)
            hit = jnp.broadcast_to(high_ref[slot : slot + 1, :], (16, 128)) == which16
            base = 160 * view + 80 * (k % 2) + k // 2
            for part, source in enumerate((coarse_ref, fine_ref)):
                for f in range(ROWS):
                    row = source[base + 8 * f : base + 8 * f + 1, :]
                    row = jnp.broadcast_to(row, (16, 128))
                    at = 144 * part + 16 * f
                    spread_ref[at : at + 16, lanes] = jnp.where(hit, row, 0.0).astype(bf16)
            hot = jnp.broadcast_to(low_ref[slot : slot + 1, :], (256, 128)) == which256
            hot_ref[:, lanes] = jnp.where(hot, 1.0, 0.0).astype(bf16)
        total = lax.dot_general(
            spread_ref[...], hot_ref[...], (((1,), (1,)), ((), ())), preferred_element_type=f32
        )
        total = total[0:144] + total[144:288]
        grads = [total[16 * f : 16 * f + 16] for f in range(ROWS)]

        right, upward, _ = camera(view)
        tanh_x, tanh_y, along_right, along_up, (c0, c1, c2) = view_geometry(rows, scaled, view)
        by_x = grads[0] * (6.0 * (1.0 - tanh_x * tanh_x))
        by_y = grads[1] * (6.0 * (1.0 - tanh_y * tanh_y))
        g0, g1, g2 = grads[2:5]
        by_xx = -(g0 * c0 * c0 + g1 * c0 * c1 + g2 * c1 * c1)
        by_xy = -(2.0 * g0 * c0 * c1 + g1 * (c0 * c2 + c1 * c1) + 2.0 * g2 * c1 * c2)
        by_yy = -(g0 * c1 * c1 + g1 * c1 * c2 + g2 * c2 * c2)
        for i in range(3):
            if right[i] != 0.0:
                by_position[i] = by_position[i] + by_x * right[i]
            by_position[i] = by_position[i] + by_y * upward[i]
        for k in range(3):
            by_right = 2.0 * by_xx * along_right[k] + by_xy * along_up[k]
            by_up = 2.0 * by_yy * along_up[k] + by_xy * along_right[k]
            by_extent[k] = by_extent[k] + by_right * along_right[k] + by_up * along_up[k]
            for i in range(3):
                if right[i] != 0.0:
                    by_rotation[i][k] = by_rotation[i][k] + by_right * right[i]
                by_rotation[i][k] = by_rotation[i][k] + by_up * upward[i]
        by_opacity = by_opacity + grads[5]
        by_color += grads[6:9]

    r = [[by_rotation[i][k] * (focal_length * extent[k]) for k in range(3)] for i in range(3)]
    by_unit = [
        2.0 * (z * (r[1][0] - r[0][1]) + y * (r[0][2] - r[2][0]) + x * (r[2][1] - r[1][2])),
        2.0
        * (
            y * (r[0][1] + r[1][0])
            + z * (r[0][2] + r[2][0])
            + w * (r[2][1] - r[1][2])
            - 2.0 * x * (r[1][1] + r[2][2])
        ),
        2.0
        * (
            x * (r[0][1] + r[1][0])
            + z * (r[1][2] + r[2][1])
            + w * (r[0][2] - r[2][0])
            - 2.0 * y * (r[0][0] + r[2][2])
        ),
        2.0
        * (
            x * (r[0][2] + r[2][0])
            + y * (r[1][2] + r[2][1])
            + w * (r[1][0] - r[0][1])
            - 2.0 * z * (r[0][0] + r[1][1])
        ),
    ]
    unit = (w, x, y, z)
    along = sum(unit[i] * by_unit[i] for i in range(4))
    by_quaternion = [(by_unit[i] - unit[i] * along) / norm for i in range(4)]
    by_logit = by_opacity * opacity * (1.0 - opacity)
    pieces = by_color + [zero] * 4 + by_position + by_extent + by_quaternion + [by_logit]
    pieces += [zero] * 5
    for n, piece in enumerate(pieces):
        stack_ref[n : n + 1, :] = piece.reshape(1, 4096)

    gradient = jnp.dot(
        spread_table_ref[...], stack_ref[...], precision=HIGHEST, preferred_element_type=f32
    )[0:59]
    new_first = beta_first * first_ref[...] + (1.0 - beta_first) * gradient
    new_second = beta_second * second_ref[...] + (1.0 - beta_second) * gradient * gradient
    new_first_ref[...] = new_first
    new_second_ref[...] = new_second
    corrected_first = new_first * (1.0 / (1.0 - beta_first**adam_step))
    corrected_second = new_second * (1.0 / (1.0 - beta_second**adam_step))
    new_params_ref[...] = params_ref[...] - learning_rate * corrected_first / (
        jnp.sqrt(corrected_second) + adam_epsilon
    )


def shards(params, first_moment, second_moment, send_table, tile_lists, list_length, target):
    devices = lax.axis_size("dev")
    table = send_table.reshape(128, 64)
    payload = jax.ShapeDtypeStruct((128, 1, PAYLOAD), f32)
    sent = pl.pallas_call(
        project_kernel,
        out_shape=payload,
        scratch_shapes=[
            pltpu.VMEM((VIEWS * ROWS, 32, 128), f32),
            pltpu.VMEM((PAYLOAD, 128), f32),
        ],
        compiler_params=pltpu.CompilerParams(vmem_limit_bytes=32 * 2**20),
        name="project",
    )(params, table, jnp.asarray(basis_table(), f32))
    arrived = lax.all_to_all(sent, "dev", split_axis=0, concat_axis=0, tiled=True)
    slopes = pl.pallas_call(
        render_kernel,
        out_shape=payload,
        scratch_shapes=[
            pltpu.VMEM((PAYLOAD, 128), f32),
            pltpu.VMEM((ROWS, 64, 128), f32),
            pltpu.VMEM((ROWS + 1, 128, 128), f32),
            pltpu.VMEM((128, 16, 8, 128), f32),
            pltpu.VMEM((128, 16, 8, 128), f32),
            pltpu.VMEM((3, 128, 128), f32),
            pltpu.VMEM((ROWS, 128, 8, 128), f32),
            pltpu.VMEM((ROWS, 128, 128), f32),
            pltpu.VMEM((160, 2048), bf16),
            pltpu.VMEM((256, 2048), bf16),
            pltpu.VMEM((160, 256), f32),
        ],
        compiler_params=pltpu.CompilerParams(vmem_limit_bytes=48 * 2**20),
        name="render",
    )(arrived, tile_lists, list_length.reshape(1, 64), target, jnp.asarray(window_matrix()))
    returned = lax.all_to_all(slopes, "dev", split_axis=0, concat_axis=0, tiled=True)
    whole = jax.ShapeDtypeStruct(params.shape, f32)
    new_params, new_first, new_second, mean_loss = pl.pallas_call(
        functools.partial(update_kernel, 3.0 * target.shape[1] * 256 * devices),
        out_shape=(whole, whole, whole, jax.ShapeDtypeStruct((1, 1), f32)),
        scratch_shapes=[
            pltpu.VMEM((PAYLOAD, 128), f32),
            pltpu.VMEM((PAYLOAD, 128), f32),
            pltpu.VMEM((64, 128), i32),
            pltpu.VMEM((64, 128), i32),
            pltpu.VMEM((288, 2048), bf16),
            pltpu.VMEM((256, 2048), bf16),
            pltpu.VMEM((32, 4096), f32),
        ],
        compiler_params=pltpu.CompilerParams(vmem_limit_bytes=48 * 2**20),
        name="update",
    )(
        returned,
        table,
        jnp.asarray(spread_table()),
        params,
        first_moment,
        second_moment,
    )
    return new_params, new_first, new_second, mean_loss.reshape(())


def solution(mesh):
    placed = (
        P(None, "dev"),
        P(None, "dev"),
        P(None, "dev"),
        P("dev", None, None),
        P("dev", None),
        P("dev"),
        P(None, "dev", None),
    )
    return jax.shard_map(
        shards,
        mesh=mesh,
        in_specs=placed,
        out_specs=(P(None, "dev"), P(None, "dev"), P(None, "dev"), P()),
        check_vma=False,
    )
```

```python
import functools
import math

import jax
import jax.numpy as jnp
import numpy as np
from jax import lax
from jax.experimental import pallas as pl
from jax.experimental.pallas import tpu as pltpu
from jax.sharding import PartitionSpec as P

VIEWS = 4
CAPV = 16
ROWS = 9
PAYLOAD = 640
VMEM_BYTES = 48 * 2**20

focal_length = 40.0
camera_pitch = 0.35
dilation = 0.3
window_sigma = 1.5
stabilizer_one = 0.0001
stabilizer_two = 0.0009
loss_blend = 0.2
beta_first = 0.9
beta_second = 0.999
adam_step = 100.0
learning_rate = 0.001
adam_epsilon = 1e-08
log2e = math.log2(math.e)
harmonic_zero = 0.28209479177387814
harmonic_one = 0.4886025119029199
harmonic_two = [
    1.0925484305920792,
    -1.0925484305920792,
    0.31539156525252005,
    -1.0925484305920792,
    0.5462742152960396,
]
harmonic_three = [
    -0.5900435899266435,
    2.890611442640554,
    -0.4570457994644658,
    0.3731763325901154,
    -0.4570457994644658,
    1.445305721320277,
    -0.5900435899266435,
]
f32 = jnp.float32
bf16 = jnp.bfloat16
i32 = jnp.int32
HIGHEST = lax.Precision.HIGHEST


def harmonics(look_x, look_y, look_z):
    xx = look_x * look_x
    yy = look_y * look_y
    zz = look_z * look_z
    return [
        harmonic_zero,
        -harmonic_one * look_y,
        harmonic_one * look_z,
        -harmonic_one * look_x,
        harmonic_two[0] * look_x * look_y,
        harmonic_two[1] * look_y * look_z,
        harmonic_two[2] * (2.0 * zz - xx - yy),
        harmonic_two[3] * look_x * look_z,
        harmonic_two[4] * (xx - yy),
        harmonic_three[0] * look_y * (3.0 * xx - yy),
        harmonic_three[1] * look_x * look_y * look_z,
        harmonic_three[2] * look_y * (4.0 * zz - xx - yy),
        harmonic_three[3] * look_z * (2.0 * zz - 3.0 * xx - 3.0 * yy),
        harmonic_three[4] * look_x * (4.0 * zz - xx - yy),
        harmonic_three[5] * look_z * (xx - yy),
        harmonic_three[6] * look_x * (xx - 3.0 * yy),
    ]


def camera(view):
    yaw = 2.0 * math.pi * view / VIEWS + 0.3
    cy, sy = math.cos(yaw), math.sin(yaw)
    cp, sp = math.cos(camera_pitch), math.sin(camera_pitch)
    return (cy, 0.0, -sy), (sp * sy, cp, sp * cy), (cp * sy, -sp, cp * cy)


def basis_table():
    table = np.zeros((16, 59), np.float64)
    for view in range(VIEWS):
        basis = harmonics(*camera(view)[2])
        for k in range(16):
            for channel in range(3):
                table[3 * view + channel, 11 + 3 * k + channel] = basis[k]
    return table


def split(values):
    high = values.astype(bf16).astype(f32)
    rest = values - high
    middle = rest.astype(bf16).astype(f32)
    return high, middle, rest - middle


def spread_table():
    table = np.zeros((64, 32), np.float64)
    table[:59, :16] = basis_table().T
    for row in range(11):
        table[row, 16 + row] = 1.0
    table = table.astype(np.float32)
    high = table.astype(bf16).astype(np.float32)
    middle = (table - high).astype(bf16).astype(np.float32)
    low = table - high - middle
    return np.concatenate([high] * 3 + [middle] * 2 + [low], axis=1).astype(bf16)


def window_matrix():
    offsets = np.arange(11) - 5.0
    normalizer = np.sum(np.exp(-offsets * offsets / (2.0 * window_sigma**2)))
    distance = np.arange(16)[:, None] - np.arange(16)[None, :]
    table = np.exp(-distance * distance / (2.0 * window_sigma**2)) / normalizer
    table = np.where(np.abs(distance) <= 5, table, 0.0)
    return np.kron(table, table).astype(np.float32)


def dot(table, axis):
    total = None
    for entry, weight in zip(table, axis):
        if weight != 0.0:
            total = entry * weight if total is None else total + entry * weight
    return total


def geometry(rows):
    extent = [jnp.exp(rows[3 + k]) for k in range(3)]
    norm = jnp.sqrt(
        rows[6] * rows[6] + rows[7] * rows[7] + rows[8] * rows[8] + rows[9] * rows[9]
    )
    w, x, y, z = (rows[6 + i] / norm for i in range(4))
    rotation = [
        [1.0 - 2.0 * (y * y + z * z), 2.0 * (x * y - w * z), 2.0 * (x * z + w * y)],
        [2.0 * (x * y + w * z), 1.0 - 2.0 * (x * x + z * z), 2.0 * (y * z - w * x)],
        [2.0 * (x * z - w * y), 2.0 * (y * z + w * x), 1.0 - 2.0 * (x * x + y * y)],
    ]
    scaled = [[focal_length * extent[k] * rotation[i][k] for k in range(3)] for i in range(3)]
    return extent, norm, (w, x, y, z), scaled


def view_geometry(rows, scaled, view):
    right, upward, _ = camera(view)
    tanh_x = jnp.tanh(dot(rows[0:3], right))
    tanh_y = jnp.tanh(dot(rows[0:3], upward))
    along_right = [dot([scaled[i][k] for i in range(3)], right) for k in range(3)]
    along_up = [dot([scaled[i][k] for i in range(3)], upward) for k in range(3)]
    spread_xx = sum(along_right[k] * along_right[k] for k in range(3)) + dilation
    spread_xy = sum(along_right[k] * along_up[k] for k in range(3))
    spread_yy = sum(along_up[k] * along_up[k] for k in range(3)) + dilation
    inverse = 1.0 / (spread_xx * spread_yy - spread_xy * spread_xy)
    conic = (spread_yy * inverse, -spread_xy * inverse, spread_xx * inverse)
    return tanh_x, tanh_y, along_right, along_up, conic


def iota(shape, dim, kind=i32):
    return lax.broadcasted_iota(i32, shape, dim).astype(kind)


def one_hot(keys, out_ref):
    which = iota((256, 128), 0)
    for i in range(64):
        hot = jnp.broadcast_to(keys[i : i + 1, :], (256, 128)) == which
        at = 128 * (i % 16)
        out_ref[i // 16, :, at : at + 128] = jnp.where(hot, 1.0, 0.0).astype(bf16)


def project_kernel(
    params_ref, table_ref, basis_ref, out_ref, held_ref, hot_ref, rows_ref, found_ref, packed_ref, sem
):
    copy = pltpu.make_async_copy(params_ref, held_ref, sem)
    copy.start()
    slots = table_ref[...]
    high = lax.shift_right_logical(slots, 8)
    one_hot(slots & 255, hot_ref)
    copy.wait()

    lead = held_ref[0:16, :].reshape(16, 16, 256)
    rows = [lead[i] for i in range(11)]
    colors = jnp.dot(
        basis_ref[...], held_ref[...], precision=HIGHEST, preferred_element_type=f32
    )
    colors = 0.5 + colors.reshape(16, 16, 256)
    _, _, _, scaled = geometry(rows)
    opacity = 1.0 / (1.0 + jnp.exp(-rows[10]))
    packed_ref[576:640, :] = jnp.zeros((64, 128), f32)
    which16 = iota((16, 128), 0)
    for view in range(VIEWS):
        tanh_x, tanh_y, _, _, conic = view_geometry(rows, scaled, view)
        projected = [8.0 + 6.0 * tanh_x, 8.0 + 6.0 * tanh_y, *conic, opacity]
        projected += [colors[3 * view + channel] for channel in range(3)]
        for half in range(2):
            lanes = slice(128 * half, 128 * half + 128)
            for f in range(8):
                rows_ref[half, pl.ds(f, 16, stride=8), :] = projected[f][:, lanes]
            rows_ref[half, 128:144, :] = projected[8][:, lanes]
        found_ref[...] = jnp.dot(
            jnp.concatenate([rows_ref[0], rows_ref[1]], axis=1).astype(bf16),
            hot_ref[view],
            preferred_element_type=f32,
        )
        for k in range(CAPV):
            lanes = slice(128 * k, 128 * k + 128)
            block = high[view * CAPV + k : view * CAPV + k + 1, :]
            block8 = jnp.broadcast_to(block, (8, 128))
            taken = found_ref[0:8, lanes]
            for h in range(1, 16):
                taken = jnp.where(block8 == h, found_ref[8 * h : 8 * h + 8, lanes], taken)
            group = 2 * view + k % 2
            at = 64 * group + 8 * (k // 2)
            packed_ref[at : at + 8, :] = taken
            here = jnp.broadcast_to(block, (16, 128)) == which16
            last = jnp.where(here, found_ref[128:144, lanes], 0.0)
            at = 512 + 8 * group + k // 2
            packed_ref[at : at + 1, :] = jnp.sum(last, axis=0, keepdims=True)
    out_ref[:, 0, :] = packed_ref[...].T


def window_mean(fields, window):
    count = len(fields)
    means = jnp.dot(
        jnp.concatenate(fields, axis=0), window, precision=HIGHEST, preferred_element_type=f32
    )
    return [means[192 * n : 192 * n + 192] for n in range(count)]


def render_kernel(
    rows_ref,
    lists_ref,
    length_ref,
    target_hbm,
    window_hbm,
    out_ref,
    target_ref,
    window_ref,
    hot_ref,
    table_ref,
    slots_ref,
    first_ref,
    ninth_ref,
    entry_ref,
    column_ref,
    cover_ref,
    weight_ref,
    image_ref,
    partial_ref,
    moment_ref,
    spread_ref,
    total_ref,
    sems,
):
    pairs = (
        (target_hbm, target_ref),
        (window_hbm, window_ref),
    )
    later_copies = [
        pltpu.make_async_copy(source, target, sems.at[n])
        for n, (source, target) in enumerate(pairs)
    ]
    for copy in later_copies:
        copy.start()
    lists = lists_ref[...]
    one_hot((lists & 1) * 128 + lax.shift_right_logical(lists, 6), hot_ref)
    slot = lists & 63
    strays = jnp.where(lax.shift_right_logical(slot, 4) != iota((64, 128), 0) // 16, 1, 0)
    regular = jnp.max(strays) == 0
    which8 = iota((8, 128), 0)

    slots_ref[...] = rows_ref[:, 0, :].T
    first_ref[...] = jnp.zeros((512, 128), f32)
    ninth_ref[...] = jnp.zeros((64, 128), f32)
    for view in range(VIEWS):
        at, at9 = 128 * view, 512 + 16 * view
        table_ref[view] = jnp.concatenate(
            [
                jnp.concatenate([slots_ref[at : at + 64], slots_ref[at + 64 : at + 128]], axis=1),
                jnp.concatenate([slots_ref[at9 : at9 + 8], slots_ref[at9 + 8 : at9 + 16]], axis=1),
                jnp.zeros((8, 256), f32),
            ],
            axis=0,
        ).astype(bf16)
    for b in range(VIEWS):
        first = jnp.where(regular, b, 0)
        last = jnp.where(regular, b + 1, VIEWS)

        def fetch(view, carry, b=b):
            found = jnp.dot(table_ref[view], hot_ref[b], preferred_element_type=f32)
            for t in range(16):
                tile = b * 16 + t
                lanes = slice(128 * t, 128 * t + 128)
                pair = lax.shift_right_logical(lists_ref[tile : tile + 1, :] & 63, 1)
                pair = jnp.broadcast_to(pair, (8, 128)) - view * 8
                taken = first_ref[8 * tile : 8 * tile + 8, :]
                for k in range(8):
                    taken = jnp.where(pair == k, found[8 * k : 8 * k + 8, lanes], taken)
                first_ref[8 * tile : 8 * tile + 8, :] = taken
                ninth = jnp.where(pair == which8, found[64:72, lanes], 0.0)
                ninth_ref[tile : tile + 1, :] += jnp.sum(ninth, axis=0, keepdims=True)
            return carry

        lax.fori_loop(first, last, fetch, 0)

    length = jnp.concatenate([length_ref[...], length_ref[...]], axis=1)
    live = iota((128, 128), 0) < length
    for f in range(ROWS):
        own = first_ref[pl.ds(f, 64, stride=8), :] if f < 8 else ninth_ref[...]
        both = jnp.concatenate([own, own], axis=0).T
        column_ref[f] = both
        if f == 5:
            column_ref[ROWS] = jnp.where(live, both, 0.0)

    lane = iota((8, 128), 1)
    base_y = jnp.where(lane < 64, 0.5, 8.5)

    def entry_row(f, j):
        return jnp.broadcast_to(column_ref[f, pl.ds(j, 1), :], (8, 128))

    for half in range(2):
        place_x = iota((8, 128), 0, f32) + (8.0 * half + 0.5)

        def forward(j, carry, half=half, place_x=place_x):
            clear, image = carry
            clear, image = list(clear), [list(c) for c in image]
            dx = place_x - entry_row(0, j)
            dy = base_y - entry_row(1, j)
            conic0 = entry_row(2, j) * (-0.5 * log2e)
            conic1 = entry_row(3, j) * (-log2e)
            conic2 = entry_row(4, j) * (-0.5 * log2e)
            opacity = entry_row(ROWS, j)
            color = [entry_row(6 + c, j) for c in range(3)]
            cross = conic1 * dx
            exponent = conic0 * dx * dx + dy * (cross + conic2 * dy)
            slope = cross + conic2 * (2.0 * dy + 1.0)
            bend = 2.0 * conic2
            for y in range(8):
                coverage = opacity * jnp.exp2(exponent)
                weight = clear[y] * coverage
                clear[y] = clear[y] - weight
                for c in range(3):
                    image[c][y] = image[c][y] + weight * color[c]
                cover_ref[j, 2 * y + half] = coverage
                weight_ref[j, 2 * y + half] = weight
                if y < 7:
                    exponent = exponent + slope
                    slope = slope + bend
            return clear, image

        zero = jnp.zeros((8, 128), f32)
        start = ([jnp.ones((8, 128), f32)] * 8, [[zero] * 8] * 3)
        _, image = lax.fori_loop(0, 128, forward, start, unroll=4)
        for c in range(3):
            for y in range(8):
                image_ref[c, 16 * y + 8 * half : 16 * y + 8 * half + 8, :] = image[c][y]

    for copy in later_copies:
        copy.wait()
    shown = []
    for c in range(3):
        turned = image_ref[c].T
        shown.append(jnp.concatenate([turned[0:64], turned[64:128]], axis=1))
    shown = jnp.concatenate(shown, axis=0)
    goal = target_ref[...].reshape(192, 256)
    fields = [shown, shown * shown, shown * goal, goal, goal * goal]
    mean_x, square_x, product, mean_y, square_y = window_mean(fields, window_ref[...])
    var_x = square_x - mean_x * mean_x
    var_y = square_y - mean_y * mean_y
    covariance = product - mean_x * mean_y
    top_one = 2.0 * mean_x * mean_y + stabilizer_one
    top_two = 2.0 * covariance + stabilizer_two
    under_one = 1.0 / (mean_x * mean_x + mean_y * mean_y + stabilizer_one)
    under_two = 1.0 / (var_x + var_y + stabilizer_two)
    under = under_one * under_two
    similarity = top_one * top_two * under
    difference = shown - goal
    pixel_loss = (1.0 - loss_blend) * jnp.abs(difference) + loss_blend * (1.0 - similarity)
    loss = jnp.sum(pixel_loss)
    by_product = 2.0 * top_one * under
    by_square = -similarity * under_two
    by_mean = (
        2.0 * mean_y * top_two * under
        - 2.0 * mean_x * similarity * under_one
        - mean_y * by_product
        - 2.0 * mean_x * by_square
    )
    by_mean, by_square, by_product = window_mean([by_mean, by_square, by_product], window_ref[...])
    slope = (1.0 - loss_blend) * jnp.where(
        difference > 0.0, 1.0, jnp.where(difference < 0.0, -1.0, 0.0)
    ) - loss_blend * (by_mean + 2.0 * shown * by_square + goal * by_product)
    for c in range(3):
        own = slope[64 * c : 64 * c + 64]
        image_ref[c] = jnp.concatenate([own[:, 0:128], own[:, 128:256]], axis=0).T

    for half in range(2):
        place_x = iota((8, 128), 0, f32) + (8.0 * half - 7.5)
        slope = [
            [image_ref[c, 16 * y + 8 * half : 16 * y + 8 * half + 8, :] for y in range(8)]
            for c in range(3)
        ]

        def backward(i, behind, half=half, place_x=place_x, slope=slope):
            j = 127 - i
            behind = list(behind)
            color = [entry_row(6 + c, j) for c in range(3)]
            by_color = [None] * 3
            sum0 = sum1 = sum2 = None
            for y in range(7, -1, -1):
                coverage = cover_ref[j, 2 * y + half]
                weight = weight_ref[j, 2 * y + half]
                own = slope[0][y] * color[0] + slope[1][y] * color[1] + slope[2][y] * color[2]
                excess = own - behind[y]
                behind[y] = behind[y] + coverage * excess
                push = weight * excess
                for c in range(3):
                    term = weight * slope[c][y]
                    by_color[c] = term if by_color[c] is None else by_color[c] + term
                sum0 = push if sum0 is None else sum0 + push
                if y > 0:
                    sum1 = sum0 if sum1 is None else sum1 + sum0
                    sum2 = sum1 if sum2 is None else sum2 + sum1
            along = sum0 * place_x
            parts = [sum0, along, along * place_x, sum1, sum1 * place_x, sum2, *by_color]
            if half == 0:
                for n in range(ROWS):
                    partial_ref[n, j] = parts[n]
            else:
                for n in range(ROWS):
                    whole = jnp.sum(parts[n] + partial_ref[n, j], axis=0, keepdims=True)
                    moment_ref[n, pl.ds(j, 1), :] = whole
            return behind

        lax.fori_loop(0, 128, backward, [jnp.zeros((8, 128), f32)] * 8, unroll=4)

    at_x = 8.0 - column_ref[0]
    at_y = jnp.where(iota((128, 128), 1) < 64, 0.5, 8.5) - column_ref[1]
    m, mx, mxx = moment_ref[0], moment_ref[1], moment_ref[2]
    my, mxy = moment_ref[3], moment_ref[4]
    myy = 2.0 * moment_ref[5] - my
    about_x = mx + at_x * m
    about_y = my + at_y * m
    about_xx = mxx + at_x * (mx + about_x)
    about_yy = myy + at_y * (my + about_y)
    about_xy = mxy + at_y * mx + at_x * about_y
    conic0, conic1, conic2 = column_ref[2], column_ref[3], column_ref[4]
    grads = [
        conic0 * about_x + conic1 * about_y,
        conic2 * about_y + conic1 * about_x,
        -0.5 * about_xx,
        -about_xy,
        -0.5 * about_yy,
        m / column_ref[5],
        moment_ref[6],
        moment_ref[7],
        moment_ref[8],
    ]
    for f in range(ROWS):
        both = grads[f].T
        whole = both[0:64] + both[64:128]
        coarse = whole.astype(bf16).astype(f32)
        entry_ref[f] = coarse
        moment_ref[f, 0:64, :] = whole - coarse

    nothing = jnp.zeros((8, 128), f32)
    for view in range(VIEWS):
        first = jnp.where(regular, view, 0)
        last = jnp.where(regular, view + 1, VIEWS)
        total_ref[...] = jnp.zeros((160, 256), f32)

        def block(b, carry, view=view):
            for t in range(16):
                tile = b * 16 + t
                here = lists_ref[pl.ds(tile, 1), :]
                pair = lax.shift_right_logical(here & 63, 1)
                hit = jnp.broadcast_to(pair, (8, 128)) == which8 + view * 8
                lanes = slice(128 * t, 128 * t + 128)
                for part, source in enumerate((entry_ref, moment_ref)):
                    pieces = []
                    for f in range(ROWS):
                        row = jnp.broadcast_to(source[f, pl.ds(tile, 1), :], (8, 128))
                        pieces.append(jnp.where(hit, row, 0.0))
                    pieces.append(nothing)
                    spread_ref[80 * part : 80 * part + 80, lanes] = jnp.concatenate(
                        pieces, axis=0
                    ).astype(bf16)
            total_ref[...] += lax.dot_general(
                spread_ref[...],
                hot_ref[b],
                (((1,), (1,)), ((), ())),
                preferred_element_type=f32,
            )
            return carry

        lax.fori_loop(first, last, block, 0)
        total = total_ref[0:80, :] + total_ref[80:160, :]
        for parity in range(2):
            at = 160 * view + 80 * parity
            slots_ref[at : at + 72, :] = total[0:72, 128 * parity : 128 * parity + 128]
            slots_ref[at + 72 : at + 80, :] = jnp.full((8, 128), loss, f32)
    out_ref[:, 0, :] = slots_ref[...].T


FACTORS = 11 * VIEWS + 9


def factors(params_ref, factor_ref):
    lead = params_ref[0:16, :].reshape(16, 16, 256)
    rows = [lead[i] for i in range(11)]
    extent, norm, unit, scaled = geometry(rows)
    opacity = 1.0 / (1.0 + jnp.exp(-rows[10]))
    for view in range(VIEWS):
        tanh_x, tanh_y, along_right, along_up, conic = view_geometry(rows, scaled, view)
        parts = [6.0 * (1.0 - tanh_x * tanh_x), 6.0 * (1.0 - tanh_y * tanh_y)]
        parts += [*along_right, *along_up, *conic]
        for n, part in enumerate(parts):
            factor_ref[11 * view + n] = part
    parts = [*unit, 1.0 / norm, *(focal_length * e for e in extent), opacity * (1.0 - opacity)]
    for n, part in enumerate(parts):
        factor_ref[11 * VIEWS + n] = part


def update_kernel(
    pixels,
    grads_ref,
    table_ref,
    spread_table_ref,
    params_hbm,
    first_hbm,
    second_hbm,
    new_params_ref,
    new_first_ref,
    new_second_ref,
    loss_ref,
    hot_ref,
    factor_ref,
    params_ref,
    first_ref,
    second_ref,
    coarse_ref,
    fine_ref,
    spread_ref,
    stack_ref,
    gradient_ref,
    result_ref,
    in_sems,
    sems,
):
    pairs = (
        (params_hbm, params_ref),
        (first_hbm, first_ref),
        (second_hbm, second_ref),
    )
    adam_copies = [
        pltpu.make_async_copy(source, target, in_sems.at[n])
        for n, (source, target) in enumerate(pairs)
    ]
    for copy in adam_copies:
        copy.start()
    one_hot(table_ref[...] & 255, hot_ref)
    adam_copies[0].wait()
    factors(params_ref, factor_ref)
    packed = grads_ref[:, 0, :].T
    loss_ref[...] = jnp.sum(packed[72:73, :], axis=1, keepdims=True) * (1.0 / pixels)
    coarse = packed.astype(bf16).astype(f32)
    coarse_ref[...] = coarse
    fine_ref[...] = packed - coarse
    high = lax.shift_right_logical(table_ref[...], 8)
    which16 = iota((16, 128), 0)

    zero = jnp.zeros((16, 256), f32)
    by_position = [zero] * 3
    by_extent = [zero] * 3
    by_rotation = [[zero] * 3 for _ in range(3)]
    by_opacity = zero
    by_color = []
    for view in range(VIEWS):
        for k in range(CAPV):
            slot = view * CAPV + k
            lanes = slice(128 * k, 128 * k + 128)
            hit = jnp.broadcast_to(high[slot : slot + 1, :], (16, 128)) == which16
            base = 160 * view + 80 * (k % 2) + k // 2
            for part, source in enumerate((coarse_ref, fine_ref)):
                for f in range(ROWS):
                    row = source[base + 8 * f : base + 8 * f + 1, :]
                    row = jnp.broadcast_to(row, (16, 128))
                    at = 144 * part + 16 * f
                    spread_ref[at : at + 16, lanes] = jnp.where(hit, row, 0.0).astype(bf16)
        total = lax.dot_general(
            spread_ref[...],
            hot_ref[view],
            (((1,), (1,)), ((), ())),
            preferred_element_type=f32,
        )
        total = total[0:144] + total[144:288]
        grads = [total[16 * f : 16 * f + 16] for f in range(ROWS)]

        right, upward, _ = camera(view)
        factor = [factor_ref[11 * view + n] for n in range(11)]
        along_right, along_up, (c0, c1, c2) = factor[2:5], factor[5:8], factor[8:11]
        by_x = grads[0] * factor[0]
        by_y = grads[1] * factor[1]
        g0, g1, g2 = grads[2:5]
        by_xx = -(g0 * c0 * c0 + g1 * c0 * c1 + g2 * c1 * c1)
        by_xy = -(2.0 * g0 * c0 * c1 + g1 * (c0 * c2 + c1 * c1) + 2.0 * g2 * c1 * c2)
        by_yy = -(g0 * c1 * c1 + g1 * c1 * c2 + g2 * c2 * c2)
        for i in range(3):
            if right[i] != 0.0:
                by_position[i] = by_position[i] + by_x * right[i]
            by_position[i] = by_position[i] + by_y * upward[i]
        for k in range(3):
            by_right = 2.0 * by_xx * along_right[k] + by_xy * along_up[k]
            by_up = 2.0 * by_yy * along_up[k] + by_xy * along_right[k]
            by_extent[k] = by_extent[k] + by_right * along_right[k] + by_up * along_up[k]
            for i in range(3):
                if right[i] != 0.0:
                    by_rotation[i][k] = by_rotation[i][k] + by_right * right[i]
                by_rotation[i][k] = by_rotation[i][k] + by_up * upward[i]
        by_opacity = by_opacity + grads[5]
        by_color += grads[6:9]

    w, x, y, z, by_norm, *scale, by_sigmoid = [factor_ref[11 * VIEWS + n] for n in range(9)]
    r = [[by_rotation[i][k] * scale[k] for k in range(3)] for i in range(3)]
    by_unit = [
        2.0 * (z * (r[1][0] - r[0][1]) + y * (r[0][2] - r[2][0]) + x * (r[2][1] - r[1][2])),
        2.0
        * (
            y * (r[0][1] + r[1][0])
            + z * (r[0][2] + r[2][0])
            + w * (r[2][1] - r[1][2])
            - 2.0 * x * (r[1][1] + r[2][2])
        ),
        2.0
        * (
            x * (r[0][1] + r[1][0])
            + z * (r[1][2] + r[2][1])
            + w * (r[0][2] - r[2][0])
            - 2.0 * y * (r[0][0] + r[2][2])
        ),
        2.0
        * (
            x * (r[0][2] + r[2][0])
            + y * (r[1][2] + r[2][1])
            + w * (r[1][0] - r[0][1])
            - 2.0 * z * (r[0][0] + r[1][1])
        ),
    ]
    unit = (w, x, y, z)
    along = sum(unit[i] * by_unit[i] for i in range(4))
    by_quaternion = [(by_unit[i] - unit[i] * along) * by_norm for i in range(4)]
    by_logit = by_opacity * by_sigmoid
    pieces = by_color + [zero] * 4 + by_position + by_extent + by_quaternion + [by_logit]
    pieces += [zero] * 5
    for n, piece in enumerate(pieces):
        stack_ref[n : n + 1, :] = piece.reshape(1, 4096)

    high, middle, low = (part.astype(bf16) for part in split(stack_ref[...]))
    gradient_ref[...] = jnp.dot(
        spread_table_ref[...],
        jnp.concatenate([high, middle, low, high, middle, high], axis=0),
        preferred_element_type=f32,
    )
    for copy in adam_copies[1:]:
        copy.wait()
    copies = []
    outs = (new_params_ref, new_first_ref, new_second_ref)
    for n, (start, stop) in enumerate(CHUNKS):
        at = slice(start, stop)
        gradient = gradient_ref[at, :]
        new_first = beta_first * first_ref[at, :] + (1.0 - beta_first) * gradient
        new_second = beta_second * second_ref[at, :] + (1.0 - beta_second) * gradient * gradient
        corrected_first = new_first * (1.0 / (1.0 - beta_first**adam_step))
        corrected_second = new_second * (1.0 / (1.0 - beta_second**adam_step))
        new_params = params_ref[at, :] - learning_rate * corrected_first / (
            jnp.sqrt(corrected_second) + adam_epsilon
        )
        for which, value in enumerate((new_params, new_first, new_second)):
            result_ref[which, at, :] = value
            copies.append(
                pltpu.make_async_copy(
                    result_ref.at[which, at, :], outs[which].at[at, :], sems.at[which, n]
                )
            )
            copies[-1].start()
    for copy in copies:
        copy.wait()


CHUNKS = ((0, 16), (16, 32), (32, 48), (48, 59))


def shards(params, first_moment, second_moment, send_table, tile_lists, list_length, target):
    devices = lax.axis_size("dev")
    table = jnp.swapaxes(send_table, 1, 2).reshape(64, 128)
    payload = jax.ShapeDtypeStruct((128, 1, PAYLOAD), f32)
    window = jnp.asarray(window_matrix())
    vmem = pl.BlockSpec(memory_space=pltpu.VMEM)
    anywhere = pl.BlockSpec(memory_space=pl.ANY)
    sent = pl.pallas_call(
        project_kernel,
        out_shape=payload,
        in_specs=[anywhere, vmem, vmem],
        scratch_shapes=[
            pltpu.VMEM((59, 4096), f32),
            pltpu.VMEM((4, 256, 2048), bf16),
            pltpu.VMEM((2, 144, 128), f32),
            pltpu.VMEM((144, 2048), f32),
            pltpu.VMEM((PAYLOAD, 128), f32),
            pltpu.SemaphoreType.DMA,
        ],
        compiler_params=pltpu.CompilerParams(vmem_limit_bytes=VMEM_BYTES),
        name="project",
    )(params, table, jnp.asarray(basis_table(), f32))
    arrived = lax.all_to_all(sent, "dev", split_axis=0, concat_axis=0, tiled=True)
    slopes = pl.pallas_call(
        render_kernel,
        out_shape=payload,
        in_specs=[vmem] * 3 + [anywhere] * 2,
        scratch_shapes=[
            pltpu.VMEM((3, 64, 256), f32),
            pltpu.VMEM((256, 256), f32),
            pltpu.VMEM((4, 256, 2048), bf16),
            pltpu.VMEM((4, 80, 256), bf16),
            pltpu.VMEM((PAYLOAD, 128), f32),
            pltpu.VMEM((512, 128), f32),
            pltpu.VMEM((64, 128), f32),
            pltpu.VMEM((ROWS, 64, 128), f32),
            pltpu.VMEM((ROWS + 1, 128, 128), f32),
            pltpu.VMEM((128, 16, 8, 128), f32),
            pltpu.VMEM((128, 16, 8, 128), f32),
            pltpu.VMEM((3, 128, 128), f32),
            pltpu.VMEM((ROWS, 128, 8, 128), f32),
            pltpu.VMEM((ROWS, 128, 128), f32),
            pltpu.VMEM((160, 2048), bf16),
            pltpu.VMEM((160, 256), f32),
            pltpu.SemaphoreType.DMA((2,)),
        ],
        compiler_params=pltpu.CompilerParams(vmem_limit_bytes=VMEM_BYTES),
        name="render",
    )(
        arrived,
        tile_lists,
        list_length.reshape(1, 64),
        target,
        window,
    )
    returned = lax.all_to_all(slopes, "dev", split_axis=0, concat_axis=0, tiled=True)
    whole = jax.ShapeDtypeStruct(params.shape, f32)
    new_params, new_first, new_second, mean_loss = pl.pallas_call(
        functools.partial(update_kernel, 3.0 * target.shape[1] * 256 * devices),
        out_shape=(whole, whole, whole, jax.ShapeDtypeStruct((1, 1), f32)),
        in_specs=[vmem] * 3 + [anywhere] * 3,
        out_specs=(anywhere, anywhere, anywhere, vmem),
        scratch_shapes=[
            pltpu.VMEM((4, 256, 2048), bf16),
            pltpu.VMEM((FACTORS, 16, 256), f32),
            pltpu.VMEM((59, 4096), f32),
            pltpu.VMEM((59, 4096), f32),
            pltpu.VMEM((59, 4096), f32),
            pltpu.VMEM((PAYLOAD, 128), f32),
            pltpu.VMEM((PAYLOAD, 128), f32),
            pltpu.VMEM((288, 2048), bf16),
            pltpu.VMEM((32, 4096), f32),
            pltpu.VMEM((64, 4096), f32),
            pltpu.VMEM((3, 59, 4096), f32),
            pltpu.SemaphoreType.DMA((3,)),
            pltpu.SemaphoreType.DMA((3, len(CHUNKS))),
        ],
        compiler_params=pltpu.CompilerParams(vmem_limit_bytes=VMEM_BYTES),
        name="update",
    )(
        returned,
        table,
        jnp.asarray(spread_table()),
        params,
        first_moment,
        second_moment,
    )
    return new_params, new_first, new_second, mean_loss.reshape(())


def solution(mesh):
    placed = (
        P(None, "dev"),
        P(None, "dev"),
        P(None, "dev"),
        P("dev", None, None),
        P("dev", None),
        P("dev"),
        P(None, "dev", None),
    )
    return jax.shard_map(
        shards,
        mesh=mesh,
        in_specs=placed,
        out_specs=(P(None, "dev"), P(None, "dev"), P(None, "dev"), P()),
        check_vma=False,
    )
```

```python
import functools
import math

import jax
import jax.numpy as jnp
import numpy as np
from jax import lax
from jax.experimental import pallas as pl
from jax.experimental.pallas import tpu as pltpu
from jax.sharding import PartitionSpec as P

VIEWS = 4
CAPV = 16
ROWS = 9
PAYLOAD = 640
VMEM_BYTES = 48 * 2**20

focal_length = 40.0
camera_pitch = 0.35
dilation = 0.3
window_sigma = 1.5
stabilizer_one = 0.0001
stabilizer_two = 0.0009
loss_blend = 0.2
beta_first = 0.9
beta_second = 0.999
adam_step = 100.0
learning_rate = 0.001
adam_epsilon = 1e-08
log2e = math.log2(math.e)
harmonic_zero = 0.28209479177387814
harmonic_one = 0.4886025119029199
harmonic_two = [
    1.0925484305920792,
    -1.0925484305920792,
    0.31539156525252005,
    -1.0925484305920792,
    0.5462742152960396,
]
harmonic_three = [
    -0.5900435899266435,
    2.890611442640554,
    -0.4570457994644658,
    0.3731763325901154,
    -0.4570457994644658,
    1.445305721320277,
    -0.5900435899266435,
]
f32 = jnp.float32
bf16 = jnp.bfloat16
i32 = jnp.int32
HIGHEST = lax.Precision.HIGHEST


def harmonics(look_x, look_y, look_z):
    xx = look_x * look_x
    yy = look_y * look_y
    zz = look_z * look_z
    return [
        harmonic_zero,
        -harmonic_one * look_y,
        harmonic_one * look_z,
        -harmonic_one * look_x,
        harmonic_two[0] * look_x * look_y,
        harmonic_two[1] * look_y * look_z,
        harmonic_two[2] * (2.0 * zz - xx - yy),
        harmonic_two[3] * look_x * look_z,
        harmonic_two[4] * (xx - yy),
        harmonic_three[0] * look_y * (3.0 * xx - yy),
        harmonic_three[1] * look_x * look_y * look_z,
        harmonic_three[2] * look_y * (4.0 * zz - xx - yy),
        harmonic_three[3] * look_z * (2.0 * zz - 3.0 * xx - 3.0 * yy),
        harmonic_three[4] * look_x * (4.0 * zz - xx - yy),
        harmonic_three[5] * look_z * (xx - yy),
        harmonic_three[6] * look_x * (xx - 3.0 * yy),
    ]


def camera(view):
    yaw = 2.0 * math.pi * view / VIEWS + 0.3
    cy, sy = math.cos(yaw), math.sin(yaw)
    cp, sp = math.cos(camera_pitch), math.sin(camera_pitch)
    return (cy, 0.0, -sy), (sp * sy, cp, sp * cy), (cp * sy, -sp, cp * cy)


def basis_table():
    table = np.zeros((16, 59), np.float64)
    for view in range(VIEWS):
        basis = harmonics(*camera(view)[2])
        for k in range(16):
            for channel in range(3):
                table[3 * view + channel, 11 + 3 * k + channel] = basis[k]
    return table


def split(values):
    high = values.astype(bf16).astype(f32)
    rest = values - high
    middle = rest.astype(bf16).astype(f32)
    return high, middle, rest - middle


def spread_table():
    table = np.zeros((64, 32), np.float64)
    table[:59, :16] = basis_table().T
    for row in range(11):
        table[row, 16 + row] = 1.0
    table = table.astype(np.float32)
    high = table.astype(bf16).astype(np.float32)
    middle = (table - high).astype(bf16).astype(np.float32)
    low = table - high - middle
    return np.concatenate([high] * 3 + [middle] * 2 + [low], axis=1).astype(bf16)


def window_matrix():
    offsets = np.arange(11) - 5.0
    normalizer = np.sum(np.exp(-offsets * offsets / (2.0 * window_sigma**2)))
    distance = np.arange(16)[:, None] - np.arange(16)[None, :]
    table = np.exp(-distance * distance / (2.0 * window_sigma**2)) / normalizer
    table = np.where(np.abs(distance) <= 5, table, 0.0)
    return np.kron(table, table).astype(np.float32)


def dot(table, axis):
    total = None
    for entry, weight in zip(table, axis):
        if weight != 0.0:
            total = entry * weight if total is None else total + entry * weight
    return total


def geometry(rows):
    extent = [jnp.exp(rows[3 + k]) for k in range(3)]
    norm = jnp.sqrt(
        rows[6] * rows[6] + rows[7] * rows[7] + rows[8] * rows[8] + rows[9] * rows[9]
    )
    w, x, y, z = (rows[6 + i] / norm for i in range(4))
    rotation = [
        [1.0 - 2.0 * (y * y + z * z), 2.0 * (x * y - w * z), 2.0 * (x * z + w * y)],
        [2.0 * (x * y + w * z), 1.0 - 2.0 * (x * x + z * z), 2.0 * (y * z - w * x)],
        [2.0 * (x * z - w * y), 2.0 * (y * z + w * x), 1.0 - 2.0 * (x * x + y * y)],
    ]
    scaled = [[focal_length * extent[k] * rotation[i][k] for k in range(3)] for i in range(3)]
    return extent, norm, (w, x, y, z), scaled


def view_geometry(rows, scaled, view):
    right, upward, _ = camera(view)
    tanh_x = jnp.tanh(dot(rows[0:3], right))
    tanh_y = jnp.tanh(dot(rows[0:3], upward))
    along_right = [dot([scaled[i][k] for i in range(3)], right) for k in range(3)]
    along_up = [dot([scaled[i][k] for i in range(3)], upward) for k in range(3)]
    spread_xx = sum(along_right[k] * along_right[k] for k in range(3)) + dilation
    spread_xy = sum(along_right[k] * along_up[k] for k in range(3))
    spread_yy = sum(along_up[k] * along_up[k] for k in range(3)) + dilation
    inverse = 1.0 / (spread_xx * spread_yy - spread_xy * spread_xy)
    conic = (spread_yy * inverse, -spread_xy * inverse, spread_xx * inverse)
    return tanh_x, tanh_y, along_right, along_up, conic


def iota(shape, dim, kind=i32):
    return lax.broadcasted_iota(i32, shape, dim).astype(kind)


def one_hot(keys, out_ref):
    which = iota((256, 128), 0)
    for i in range(64):
        hot = jnp.broadcast_to(keys[i : i + 1, :], (256, 128)) == which
        at = 128 * (i % 16)
        out_ref[i // 16, :, at : at + 128] = jnp.where(hot, 1.0, 0.0).astype(bf16)


def project_kernel(
    params_ref, table_ref, basis_ref, out_ref, held_ref, hot_ref, rows_ref, found_ref, packed_ref, sem
):
    copy = pltpu.make_async_copy(params_ref, held_ref, sem)
    copy.start()
    slots = table_ref[...]
    high = lax.shift_right_logical(slots, 8)
    one_hot(slots & 255, hot_ref)
    copy.wait()

    lead = held_ref[0:16, :].reshape(16, 16, 256)
    rows = [lead[i] for i in range(11)]
    colors = jnp.dot(
        basis_ref[...], held_ref[...], precision=HIGHEST, preferred_element_type=f32
    )
    colors = 0.5 + colors.reshape(16, 16, 256)
    _, _, _, scaled = geometry(rows)
    opacity = 1.0 / (1.0 + jnp.exp(-rows[10]))
    packed_ref[576:640, :] = jnp.zeros((64, 128), f32)
    which16 = iota((16, 128), 0)
    for view in range(VIEWS):
        tanh_x, tanh_y, _, _, conic = view_geometry(rows, scaled, view)
        projected = [8.0 + 6.0 * tanh_x, 8.0 + 6.0 * tanh_y, *conic, opacity]
        projected += [colors[3 * view + channel] for channel in range(3)]
        for half in range(2):
            lanes = slice(128 * half, 128 * half + 128)
            for f in range(8):
                rows_ref[half, pl.ds(f, 16, stride=8), :] = projected[f][:, lanes]
            rows_ref[half, 128:144, :] = projected[8][:, lanes]
        found_ref[...] = jnp.dot(
            jnp.concatenate([rows_ref[0], rows_ref[1]], axis=1).astype(bf16),
            hot_ref[view],
            preferred_element_type=f32,
        )
        for k in range(CAPV):
            lanes = slice(128 * k, 128 * k + 128)
            block = high[view * CAPV + k : view * CAPV + k + 1, :]
            block8 = jnp.broadcast_to(block, (8, 128))
            taken = found_ref[0:8, lanes]
            for h in range(1, 16):
                taken = jnp.where(block8 == h, found_ref[8 * h : 8 * h + 8, lanes], taken)
            group = 2 * view + k % 2
            at = 64 * group + 8 * (k // 2)
            packed_ref[at : at + 8, :] = taken
            here = jnp.broadcast_to(block, (16, 128)) == which16
            last = jnp.where(here, found_ref[128:144, lanes], 0.0)
            at = 512 + 8 * group + k // 2
            packed_ref[at : at + 1, :] = jnp.sum(last, axis=0, keepdims=True)
    out_ref[:, 0, :] = packed_ref[...].T


def window_mean(fields, window):
    count = len(fields)
    means = jnp.dot(
        jnp.concatenate(fields, axis=0), window, precision=HIGHEST, preferred_element_type=f32
    )
    return [means[192 * n : 192 * n + 192] for n in range(count)]


def window_mean_split(fields, window):
    field = jnp.concatenate(fields, axis=0)
    coarse, weight = field.astype(bf16), window.astype(bf16)
    fine = (field - coarse.astype(f32)).astype(bf16)
    weight_fine = (window - weight.astype(f32)).astype(bf16)
    means = jnp.dot(
        jnp.concatenate([coarse, fine, coarse], axis=1),
        jnp.concatenate([weight, weight, weight_fine], axis=0),
        preferred_element_type=f32,
    )
    return [means[192 * n : 192 * n + 192] for n in range(len(fields))]


def render_kernel(
    rows_ref,
    lists_ref,
    length_ref,
    target_hbm,
    window_hbm,
    out_ref,
    target_ref,
    window_ref,
    hot_ref,
    table_ref,
    slots_ref,
    first_ref,
    ninth_ref,
    entry_ref,
    column_ref,
    cover_ref,
    weight_ref,
    image_ref,
    partial_ref,
    moment_ref,
    spread_ref,
    total_ref,
    sems,
):
    pairs = (
        (target_hbm, target_ref),
        (window_hbm, window_ref),
    )
    later_copies = [
        pltpu.make_async_copy(source, target, sems.at[n])
        for n, (source, target) in enumerate(pairs)
    ]
    for copy in later_copies:
        copy.start()
    lists = lists_ref[...]
    one_hot((lists & 1) * 128 + lax.shift_right_logical(lists, 6), hot_ref)
    slot = lists & 63
    strays = jnp.where(lax.shift_right_logical(slot, 4) != iota((64, 128), 0) // 16, 1, 0)
    regular = jnp.max(strays) == 0
    which8 = iota((8, 128), 0)

    slots_ref[...] = rows_ref[:, 0, :].T
    first_ref[...] = jnp.zeros((512, 128), f32)
    ninth_ref[...] = jnp.zeros((64, 128), f32)
    for view in range(VIEWS):
        at, at9 = 128 * view, 512 + 16 * view
        table_ref[view] = jnp.concatenate(
            [
                jnp.concatenate([slots_ref[at : at + 64], slots_ref[at + 64 : at + 128]], axis=1),
                jnp.concatenate([slots_ref[at9 : at9 + 8], slots_ref[at9 + 8 : at9 + 16]], axis=1),
                jnp.zeros((8, 256), f32),
            ],
            axis=0,
        ).astype(bf16)
    for b in range(VIEWS):
        first = jnp.where(regular, b, 0)
        last = jnp.where(regular, b + 1, VIEWS)

        def fetch(view, carry, b=b):
            found = jnp.dot(table_ref[view], hot_ref[b], preferred_element_type=f32)
            for t in range(16):
                tile = b * 16 + t
                lanes = slice(128 * t, 128 * t + 128)
                pair = lax.shift_right_logical(lists_ref[tile : tile + 1, :] & 63, 1)
                pair = jnp.broadcast_to(pair, (8, 128)) - view * 8
                taken = first_ref[8 * tile : 8 * tile + 8, :]
                for k in range(8):
                    taken = jnp.where(pair == k, found[8 * k : 8 * k + 8, lanes], taken)
                first_ref[8 * tile : 8 * tile + 8, :] = taken
                ninth = jnp.where(pair == which8, found[64:72, lanes], 0.0)
                ninth_ref[tile : tile + 1, :] += jnp.sum(ninth, axis=0, keepdims=True)
            return carry

        lax.fori_loop(first, last, fetch, 0)

    length = jnp.concatenate([length_ref[...], length_ref[...]], axis=1)
    live = iota((128, 128), 0) < length
    for f in range(ROWS):
        own = first_ref[pl.ds(f, 64, stride=8), :] if f < 8 else ninth_ref[...]
        both = jnp.concatenate([own, own], axis=0).T
        column_ref[f] = both
        if f == 5:
            column_ref[ROWS] = jnp.where(live, both, 0.0)

    lane = iota((8, 128), 1)
    base_y = jnp.where(lane < 64, 0.5, 8.5)

    def entry_row(f, j):
        return jnp.broadcast_to(column_ref[f, pl.ds(j, 1), :], (8, 128))

    for half in range(2):
        place_x = iota((8, 128), 0, f32) + (8.0 * half + 0.5)

        def forward(j, carry, half=half, place_x=place_x):
            clear, image = carry
            clear, image = list(clear), [list(c) for c in image]
            dx = place_x - entry_row(0, j)
            dy = base_y - entry_row(1, j)
            conic0 = entry_row(2, j) * (-0.5 * log2e)
            conic1 = entry_row(3, j) * (-log2e)
            conic2 = entry_row(4, j) * (-0.5 * log2e)
            opacity = entry_row(ROWS, j)
            color = [entry_row(6 + c, j) for c in range(3)]
            cross = conic1 * dx
            exponent = conic0 * dx * dx + dy * (cross + conic2 * dy)
            slope = cross + conic2 * (2.0 * dy + 1.0)
            bend = 2.0 * conic2
            for y in range(8):
                coverage = opacity * jnp.exp2(exponent)
                weight = clear[y] * coverage
                clear[y] = clear[y] - weight
                for c in range(3):
                    image[c][y] = image[c][y] + weight * color[c]
                cover_ref[j, 2 * y + half] = coverage
                weight_ref[j, 2 * y + half] = weight
                if y < 7:
                    exponent = exponent + slope
                    slope = slope + bend
            return clear, image

        zero = jnp.zeros((8, 128), f32)
        start = ([jnp.ones((8, 128), f32)] * 8, [[zero] * 8] * 3)
        _, image = lax.fori_loop(0, 128, forward, start, unroll=8)
        for c in range(3):
            for y in range(8):
                image_ref[c, 16 * y + 8 * half : 16 * y + 8 * half + 8, :] = image[c][y]

    for copy in later_copies:
        copy.wait()
    shown = []
    for c in range(3):
        turned = image_ref[c].T
        shown.append(jnp.concatenate([turned[0:64], turned[64:128]], axis=1))
    shown = jnp.concatenate(shown, axis=0)
    goal = target_ref[...].reshape(192, 256)
    fields = [shown, shown * shown, shown * goal, goal, goal * goal]
    mean_x, square_x, product, mean_y, square_y = window_mean(fields, window_ref[...])
    var_x = square_x - mean_x * mean_x
    var_y = square_y - mean_y * mean_y
    covariance = product - mean_x * mean_y
    top_one = 2.0 * mean_x * mean_y + stabilizer_one
    top_two = 2.0 * covariance + stabilizer_two
    under_one = 1.0 / (mean_x * mean_x + mean_y * mean_y + stabilizer_one)
    under_two = 1.0 / (var_x + var_y + stabilizer_two)
    under = under_one * under_two
    similarity = top_one * top_two * under
    difference = shown - goal
    pixel_loss = (1.0 - loss_blend) * jnp.abs(difference) + loss_blend * (1.0 - similarity)
    loss = jnp.sum(pixel_loss)
    by_product = 2.0 * top_one * under
    by_square = -similarity * under_two
    by_mean = (
        2.0 * mean_y * top_two * under
        - 2.0 * mean_x * similarity * under_one
        - mean_y * by_product
        - 2.0 * mean_x * by_square
    )
    fields = [by_mean, by_square, by_product]
    by_mean, by_square, by_product = window_mean_split(fields, window_ref[...])
    slope = (1.0 - loss_blend) * jnp.where(
        difference > 0.0, 1.0, jnp.where(difference < 0.0, -1.0, 0.0)
    ) - loss_blend * (by_mean + 2.0 * shown * by_square + goal * by_product)
    for c in range(3):
        own = slope[64 * c : 64 * c + 64]
        image_ref[c] = jnp.concatenate([own[:, 0:128], own[:, 128:256]], axis=0).T

    for half in range(2):
        place_x = iota((8, 128), 0, f32) + (8.0 * half - 7.5)
        slope = [
            [image_ref[c, 16 * y + 8 * half : 16 * y + 8 * half + 8, :] for y in range(8)]
            for c in range(3)
        ]

        def backward(i, behind, half=half, place_x=place_x, slope=slope):
            j = 127 - i
            behind = list(behind)
            color = [entry_row(6 + c, j) for c in range(3)]
            by_color = [None] * 3
            sum0 = sum1 = sum2 = None
            for y in range(7, -1, -1):
                coverage = cover_ref[j, 2 * y + half]
                weight = weight_ref[j, 2 * y + half]
                own = slope[0][y] * color[0] + slope[1][y] * color[1] + slope[2][y] * color[2]
                excess = own - behind[y]
                behind[y] = behind[y] + coverage * excess
                push = weight * excess
                for c in range(3):
                    term = weight * slope[c][y]
                    by_color[c] = term if by_color[c] is None else by_color[c] + term
                sum0 = push if sum0 is None else sum0 + push
                if y > 0:
                    sum1 = sum0 if sum1 is None else sum1 + sum0
                    sum2 = sum1 if sum2 is None else sum2 + sum1
            along = sum0 * place_x
            parts = [sum0, along, along * place_x, sum1, sum1 * place_x, sum2, *by_color]
            if half == 0:
                for n in range(ROWS):
                    partial_ref[n, j] = parts[n]
            else:
                for n in range(ROWS):
                    whole = jnp.sum(parts[n] + partial_ref[n, j], axis=0, keepdims=True)
                    moment_ref[n, pl.ds(j, 1), :] = whole
            return behind

        lax.fori_loop(0, 128, backward, [jnp.zeros((8, 128), f32)] * 8, unroll=8)

    at_x = 8.0 - column_ref[0]
    at_y = jnp.where(iota((128, 128), 1) < 64, 0.5, 8.5) - column_ref[1]
    m, mx, mxx = moment_ref[0], moment_ref[1], moment_ref[2]
    my, mxy = moment_ref[3], moment_ref[4]
    myy = 2.0 * moment_ref[5] - my
    about_x = mx + at_x * m
    about_y = my + at_y * m
    about_xx = mxx + at_x * (mx + about_x)
    about_yy = myy + at_y * (my + about_y)
    about_xy = mxy + at_y * mx + at_x * about_y
    conic0, conic1, conic2 = column_ref[2], column_ref[3], column_ref[4]
    grads = [
        conic0 * about_x + conic1 * about_y,
        conic2 * about_y + conic1 * about_x,
        -0.5 * about_xx,
        -about_xy,
        -0.5 * about_yy,
        m / column_ref[5],
        moment_ref[6],
        moment_ref[7],
        moment_ref[8],
    ]
    for f in range(ROWS):
        both = grads[f].T
        whole = both[0:64] + both[64:128]
        coarse = whole.astype(bf16).astype(f32)
        entry_ref[f] = coarse
        moment_ref[f, 0:64, :] = whole - coarse

    nothing = jnp.zeros((8, 128), f32)
    for view in range(VIEWS):
        first = jnp.where(regular, view, 0)
        last = jnp.where(regular, view + 1, VIEWS)
        total_ref[...] = jnp.zeros((160, 256), f32)

        def block(b, carry, view=view):
            for t in range(16):
                tile = b * 16 + t
                here = lists_ref[pl.ds(tile, 1), :]
                pair = lax.shift_right_logical(here & 63, 1)
                hit = jnp.broadcast_to(pair, (8, 128)) == which8 + view * 8
                lanes = slice(128 * t, 128 * t + 128)
                for part, source in enumerate((entry_ref, moment_ref)):
                    pieces = []
                    for f in range(ROWS):
                        row = jnp.broadcast_to(source[f, pl.ds(tile, 1), :], (8, 128))
                        pieces.append(jnp.where(hit, row, 0.0))
                    pieces.append(nothing)
                    spread_ref[80 * part : 80 * part + 80, lanes] = jnp.concatenate(
                        pieces, axis=0
                    ).astype(bf16)
            total_ref[...] += lax.dot_general(
                spread_ref[...],
                hot_ref[b],
                (((1,), (1,)), ((), ())),
                preferred_element_type=f32,
            )
            return carry

        lax.fori_loop(first, last, block, 0)
        total = total_ref[0:80, :] + total_ref[80:160, :]
        for parity in range(2):
            at = 160 * view + 80 * parity
            slots_ref[at : at + 72, :] = total[0:72, 128 * parity : 128 * parity + 128]
            slots_ref[at + 72 : at + 80, :] = jnp.full((8, 128), loss, f32)
    out_ref[:, 0, :] = slots_ref[...].T


FACTORS = 11 * VIEWS + 9


def factors(params_ref, factor_ref):
    lead = params_ref[0:16, :].reshape(16, 16, 256)
    rows = [lead[i] for i in range(11)]
    extent, norm, unit, scaled = geometry(rows)
    opacity = 1.0 / (1.0 + jnp.exp(-rows[10]))
    for view in range(VIEWS):
        tanh_x, tanh_y, along_right, along_up, conic = view_geometry(rows, scaled, view)
        parts = [6.0 * (1.0 - tanh_x * tanh_x), 6.0 * (1.0 - tanh_y * tanh_y)]
        parts += [*along_right, *along_up, *conic]
        for n, part in enumerate(parts):
            factor_ref[11 * view + n] = part
    parts = [*unit, 1.0 / norm, *(focal_length * e for e in extent), opacity * (1.0 - opacity)]
    for n, part in enumerate(parts):
        factor_ref[11 * VIEWS + n] = part


def update_kernel(
    pixels,
    grads_ref,
    table_ref,
    spread_table_ref,
    params_hbm,
    first_hbm,
    second_hbm,
    new_params_ref,
    new_first_ref,
    new_second_ref,
    loss_ref,
    hot_ref,
    factor_ref,
    params_ref,
    first_ref,
    second_ref,
    coarse_ref,
    fine_ref,
    spread_ref,
    stack_ref,
    gradient_ref,
    result_ref,
    in_sems,
    sems,
):
    pairs = (
        (params_hbm, params_ref),
        (first_hbm, first_ref),
        (second_hbm, second_ref),
    )
    adam_copies = [
        pltpu.make_async_copy(source, target, in_sems.at[n])
        for n, (source, target) in enumerate(pairs)
    ]
    for copy in adam_copies:
        copy.start()
    one_hot(table_ref[...] & 255, hot_ref)
    adam_copies[0].wait()
    factors(params_ref, factor_ref)
    packed = grads_ref[:, 0, :].T
    loss_ref[...] = jnp.sum(packed[72:73, :], axis=1, keepdims=True) * (1.0 / pixels)
    coarse = packed.astype(bf16).astype(f32)
    coarse_ref[...] = coarse
    fine_ref[...] = packed - coarse
    high = lax.shift_right_logical(table_ref[...], 8)
    which16 = iota((16, 128), 0)

    zero = jnp.zeros((16, 256), f32)
    by_position = [zero] * 3
    by_extent = [zero] * 3
    by_rotation = [[zero] * 3 for _ in range(3)]
    by_opacity = zero
    by_color = []
    for view in range(VIEWS):
        for k in range(CAPV):
            slot = view * CAPV + k
            lanes = slice(128 * k, 128 * k + 128)
            hit = jnp.broadcast_to(high[slot : slot + 1, :], (16, 128)) == which16
            base = 160 * view + 80 * (k % 2) + k // 2
            for part, source in enumerate((coarse_ref, fine_ref)):
                for f in range(ROWS):
                    row = source[base + 8 * f : base + 8 * f + 1, :]
                    row = jnp.broadcast_to(row, (16, 128))
                    at = 144 * part + 16 * f
                    spread_ref[at : at + 16, lanes] = jnp.where(hit, row, 0.0).astype(bf16)
        total = lax.dot_general(
            spread_ref[...],
            hot_ref[view],
            (((1,), (1,)), ((), ())),
            preferred_element_type=f32,
        )
        total = total[0:144] + total[144:288]
        grads = [total[16 * f : 16 * f + 16] for f in range(ROWS)]

        right, upward, _ = camera(view)
        factor = [factor_ref[11 * view + n] for n in range(11)]
        along_right, along_up, (c0, c1, c2) = factor[2:5], factor[5:8], factor[8:11]
        by_x = grads[0] * factor[0]
        by_y = grads[1] * factor[1]
        g0, g1, g2 = grads[2:5]
        by_xx = -(g0 * c0 * c0 + g1 * c0 * c1 + g2 * c1 * c1)
        by_xy = -(2.0 * g0 * c0 * c1 + g1 * (c0 * c2 + c1 * c1) + 2.0 * g2 * c1 * c2)
        by_yy = -(g0 * c1 * c1 + g1 * c1 * c2 + g2 * c2 * c2)
        for i in range(3):
            if right[i] != 0.0:
                by_position[i] = by_position[i] + by_x * right[i]
            by_position[i] = by_position[i] + by_y * upward[i]
        for k in range(3):
            by_right = 2.0 * by_xx * along_right[k] + by_xy * along_up[k]
            by_up = 2.0 * by_yy * along_up[k] + by_xy * along_right[k]
            by_extent[k] = by_extent[k] + by_right * along_right[k] + by_up * along_up[k]
            for i in range(3):
                if right[i] != 0.0:
                    by_rotation[i][k] = by_rotation[i][k] + by_right * right[i]
                by_rotation[i][k] = by_rotation[i][k] + by_up * upward[i]
        by_opacity = by_opacity + grads[5]
        by_color += grads[6:9]

    w, x, y, z, by_norm, *scale, by_sigmoid = [factor_ref[11 * VIEWS + n] for n in range(9)]
    r = [[by_rotation[i][k] * scale[k] for k in range(3)] for i in range(3)]
    by_unit = [
        2.0 * (z * (r[1][0] - r[0][1]) + y * (r[0][2] - r[2][0]) + x * (r[2][1] - r[1][2])),
        2.0
        * (
            y * (r[0][1] + r[1][0])
            + z * (r[0][2] + r[2][0])
            + w * (r[2][1] - r[1][2])
            - 2.0 * x * (r[1][1] + r[2][2])
        ),
        2.0
        * (
            x * (r[0][1] + r[1][0])
            + z * (r[1][2] + r[2][1])
            + w * (r[0][2] - r[2][0])
            - 2.0 * y * (r[0][0] + r[2][2])
        ),
        2.0
        * (
            x * (r[0][2] + r[2][0])
            + y * (r[1][2] + r[2][1])
            + w * (r[1][0] - r[0][1])
            - 2.0 * z * (r[0][0] + r[1][1])
        ),
    ]
    unit = (w, x, y, z)
    along = sum(unit[i] * by_unit[i] for i in range(4))
    by_quaternion = [(by_unit[i] - unit[i] * along) * by_norm for i in range(4)]
    by_logit = by_opacity * by_sigmoid
    pieces = by_color + [zero] * 4 + by_position + by_extent + by_quaternion + [by_logit]
    pieces += [zero] * 5
    for n, piece in enumerate(pieces):
        stack_ref[n : n + 1, :] = piece.reshape(1, 4096)

    high, middle, low = (part.astype(bf16) for part in split(stack_ref[...]))
    gradient_ref[...] = jnp.dot(
        spread_table_ref[...],
        jnp.concatenate([high, middle, low, high, middle, high], axis=0),
        preferred_element_type=f32,
    )
    for copy in adam_copies[1:]:
        copy.wait()
    copies = []
    outs = (new_params_ref, new_first_ref, new_second_ref)
    for n, (start, stop) in enumerate(CHUNKS):
        at = slice(start, stop)
        gradient = gradient_ref[at, :]
        new_first = beta_first * first_ref[at, :] + (1.0 - beta_first) * gradient
        new_second = beta_second * second_ref[at, :] + (1.0 - beta_second) * gradient * gradient
        corrected_first = new_first * (1.0 / (1.0 - beta_first**adam_step))
        corrected_second = new_second * (1.0 / (1.0 - beta_second**adam_step))
        new_params = params_ref[at, :] - learning_rate * corrected_first / (
            jnp.sqrt(corrected_second) + adam_epsilon
        )
        for which, value in enumerate((new_params, new_first, new_second)):
            result_ref[which, at, :] = value
            copies.append(
                pltpu.make_async_copy(
                    result_ref.at[which, at, :], outs[which].at[at, :], sems.at[which, n]
                )
            )
            copies[-1].start()
    for copy in copies:
        copy.wait()


CHUNKS = ((0, 16), (16, 32), (32, 48), (48, 59))


def shards(params, first_moment, second_moment, send_table, tile_lists, list_length, target):
    devices = lax.axis_size("dev")
    table = jnp.swapaxes(send_table, 1, 2).reshape(64, 128)
    payload = jax.ShapeDtypeStruct((128, 1, PAYLOAD), f32)
    window = jnp.asarray(window_matrix())
    vmem = pl.BlockSpec(memory_space=pltpu.VMEM)
    anywhere = pl.BlockSpec(memory_space=pl.ANY)
    sent = pl.pallas_call(
        project_kernel,
        out_shape=payload,
        in_specs=[anywhere, vmem, vmem],
        scratch_shapes=[
            pltpu.VMEM((59, 4096), f32),
            pltpu.VMEM((4, 256, 2048), bf16),
            pltpu.VMEM((2, 144, 128), f32),
            pltpu.VMEM((144, 2048), f32),
            pltpu.VMEM((PAYLOAD, 128), f32),
            pltpu.SemaphoreType.DMA,
        ],
        compiler_params=pltpu.CompilerParams(vmem_limit_bytes=VMEM_BYTES),
        name="project",
    )(params, table, jnp.asarray(basis_table(), f32))
    arrived = lax.all_to_all(sent, "dev", split_axis=0, concat_axis=0, tiled=True)
    slopes = pl.pallas_call(
        render_kernel,
        out_shape=payload,
        in_specs=[vmem] * 3 + [anywhere] * 2,
        scratch_shapes=[
            pltpu.VMEM((3, 64, 256), f32),
            pltpu.VMEM((256, 256), f32),
            pltpu.VMEM((4, 256, 2048), bf16),
            pltpu.VMEM((4, 80, 256), bf16),
            pltpu.VMEM((PAYLOAD, 128), f32),
            pltpu.VMEM((512, 128), f32),
            pltpu.VMEM((64, 128), f32),
            pltpu.VMEM((ROWS, 64, 128), f32),
            pltpu.VMEM((ROWS + 1, 128, 128), f32),
            pltpu.VMEM((128, 16, 8, 128), f32),
            pltpu.VMEM((128, 16, 8, 128), f32),
            pltpu.VMEM((3, 128, 128), f32),
            pltpu.VMEM((ROWS, 128, 8, 128), f32),
            pltpu.VMEM((ROWS, 128, 128), f32),
            pltpu.VMEM((160, 2048), bf16),
            pltpu.VMEM((160, 256), f32),
            pltpu.SemaphoreType.DMA((2,)),
        ],
        compiler_params=pltpu.CompilerParams(vmem_limit_bytes=VMEM_BYTES),
        name="render",
    )(
        arrived,
        tile_lists,
        list_length.reshape(1, 64),
        target,
        window,
    )
    returned = lax.all_to_all(slopes, "dev", split_axis=0, concat_axis=0, tiled=True)
    whole = jax.ShapeDtypeStruct(params.shape, f32)
    new_params, new_first, new_second, mean_loss = pl.pallas_call(
        functools.partial(update_kernel, 3.0 * target.shape[1] * 256 * devices),
        out_shape=(whole, whole, whole, jax.ShapeDtypeStruct((1, 1), f32)),
        in_specs=[vmem] * 3 + [anywhere] * 3,
        out_specs=(anywhere, anywhere, anywhere, vmem),
        scratch_shapes=[
            pltpu.VMEM((4, 256, 2048), bf16),
            pltpu.VMEM((FACTORS, 16, 256), f32),
            pltpu.VMEM((59, 4096), f32),
            pltpu.VMEM((59, 4096), f32),
            pltpu.VMEM((59, 4096), f32),
            pltpu.VMEM((PAYLOAD, 128), f32),
            pltpu.VMEM((PAYLOAD, 128), f32),
            pltpu.VMEM((288, 2048), bf16),
            pltpu.VMEM((32, 4096), f32),
            pltpu.VMEM((64, 4096), f32),
            pltpu.VMEM((3, 59, 4096), f32),
            pltpu.SemaphoreType.DMA((3,)),
            pltpu.SemaphoreType.DMA((3, len(CHUNKS))),
        ],
        compiler_params=pltpu.CompilerParams(vmem_limit_bytes=VMEM_BYTES),
        name="update",
    )(
        returned,
        table,
        jnp.asarray(spread_table()),
        params,
        first_moment,
        second_moment,
    )
    return new_params, new_first, new_second, mean_loss.reshape(())


def solution(mesh):
    placed = (
        P(None, "dev"),
        P(None, "dev"),
        P(None, "dev"),
        P("dev", None, None),
        P("dev", None),
        P("dev"),
        P(None, "dev", None),
    )
    return jax.shard_map(
        shards,
        mesh=mesh,
        in_specs=placed,
        out_specs=(P(None, "dev"), P(None, "dev"), P(None, "dev"), P()),
        check_vma=False,
    )
```

```python
import functools
import math

import jax
import jax.numpy as jnp
import numpy as np
from jax import lax
from jax.experimental import pallas as pl
from jax.experimental.pallas import tpu as pltpu
from jax.sharding import PartitionSpec as P

VIEWS = 4
CAPV = 16
ROWS = 9
PAYLOAD = 640
VMEM_BYTES = 48 * 2**20

focal_length = 40.0
camera_pitch = 0.35
dilation = 0.3
window_sigma = 1.5
stabilizer_one = 0.0001
stabilizer_two = 0.0009
loss_blend = 0.2
beta_first = 0.9
beta_second = 0.999
adam_step = 100.0
learning_rate = 0.001
adam_epsilon = 1e-08
log2e = math.log2(math.e)
harmonic_zero = 0.28209479177387814
harmonic_one = 0.4886025119029199
harmonic_two = [
    1.0925484305920792,
    -1.0925484305920792,
    0.31539156525252005,
    -1.0925484305920792,
    0.5462742152960396,
]
harmonic_three = [
    -0.5900435899266435,
    2.890611442640554,
    -0.4570457994644658,
    0.3731763325901154,
    -0.4570457994644658,
    1.445305721320277,
    -0.5900435899266435,
]
f32 = jnp.float32
bf16 = jnp.bfloat16
i32 = jnp.int32
HIGHEST = lax.Precision.HIGHEST


def harmonics(look_x, look_y, look_z):
    xx = look_x * look_x
    yy = look_y * look_y
    zz = look_z * look_z
    return [
        harmonic_zero,
        -harmonic_one * look_y,
        harmonic_one * look_z,
        -harmonic_one * look_x,
        harmonic_two[0] * look_x * look_y,
        harmonic_two[1] * look_y * look_z,
        harmonic_two[2] * (2.0 * zz - xx - yy),
        harmonic_two[3] * look_x * look_z,
        harmonic_two[4] * (xx - yy),
        harmonic_three[0] * look_y * (3.0 * xx - yy),
        harmonic_three[1] * look_x * look_y * look_z,
        harmonic_three[2] * look_y * (4.0 * zz - xx - yy),
        harmonic_three[3] * look_z * (2.0 * zz - 3.0 * xx - 3.0 * yy),
        harmonic_three[4] * look_x * (4.0 * zz - xx - yy),
        harmonic_three[5] * look_z * (xx - yy),
        harmonic_three[6] * look_x * (xx - 3.0 * yy),
    ]


def camera(view):
    yaw = 2.0 * math.pi * view / VIEWS + 0.3
    cy, sy = math.cos(yaw), math.sin(yaw)
    cp, sp = math.cos(camera_pitch), math.sin(camera_pitch)
    return (cy, 0.0, -sy), (sp * sy, cp, sp * cy), (cp * sy, -sp, cp * cy)


def basis_table():
    table = np.zeros((16, 59), np.float64)
    for view in range(VIEWS):
        basis = harmonics(*camera(view)[2])
        for k in range(16):
            for channel in range(3):
                table[3 * view + channel, 11 + 3 * k + channel] = basis[k]
    return table


def split(values):
    high = values.astype(bf16).astype(f32)
    rest = values - high
    middle = rest.astype(bf16).astype(f32)
    return high, middle, rest - middle


def spread_table():
    table = np.zeros((64, 32), np.float64)
    table[:59, :16] = basis_table().T
    for row in range(11):
        table[row, 16 + row] = 1.0
    table = table.astype(np.float32)
    high = table.astype(bf16).astype(np.float32)
    middle = (table - high).astype(bf16).astype(np.float32)
    low = table - high - middle
    return np.concatenate([high] * 3 + [middle] * 2 + [low], axis=1).astype(bf16)


def window_matrix():
    offsets = np.arange(11) - 5.0
    normalizer = np.sum(np.exp(-offsets * offsets / (2.0 * window_sigma**2)))
    distance = np.arange(16)[:, None] - np.arange(16)[None, :]
    table = np.exp(-distance * distance / (2.0 * window_sigma**2)) / normalizer
    table = np.where(np.abs(distance) <= 5, table, 0.0)
    return np.kron(table, table).astype(np.float32)


def dot(table, axis):
    total = None
    for entry, weight in zip(table, axis):
        if weight != 0.0:
            total = entry * weight if total is None else total + entry * weight
    return total


def geometry(rows):
    extent = [jnp.exp(rows[3 + k]) for k in range(3)]
    norm = jnp.sqrt(
        rows[6] * rows[6] + rows[7] * rows[7] + rows[8] * rows[8] + rows[9] * rows[9]
    )
    w, x, y, z = (rows[6 + i] / norm for i in range(4))
    rotation = [
        [1.0 - 2.0 * (y * y + z * z), 2.0 * (x * y - w * z), 2.0 * (x * z + w * y)],
        [2.0 * (x * y + w * z), 1.0 - 2.0 * (x * x + z * z), 2.0 * (y * z - w * x)],
        [2.0 * (x * z - w * y), 2.0 * (y * z + w * x), 1.0 - 2.0 * (x * x + y * y)],
    ]
    scaled = [[focal_length * extent[k] * rotation[i][k] for k in range(3)] for i in range(3)]
    return extent, norm, (w, x, y, z), scaled


def view_geometry(rows, scaled, view):
    right, upward, _ = camera(view)
    tanh_x = jnp.tanh(dot(rows[0:3], right))
    tanh_y = jnp.tanh(dot(rows[0:3], upward))
    along_right = [dot([scaled[i][k] for i in range(3)], right) for k in range(3)]
    along_up = [dot([scaled[i][k] for i in range(3)], upward) for k in range(3)]
    spread_xx = sum(along_right[k] * along_right[k] for k in range(3)) + dilation
    spread_xy = sum(along_right[k] * along_up[k] for k in range(3))
    spread_yy = sum(along_up[k] * along_up[k] for k in range(3)) + dilation
    inverse = 1.0 / (spread_xx * spread_yy - spread_xy * spread_xy)
    conic = (spread_yy * inverse, -spread_xy * inverse, spread_xx * inverse)
    return tanh_x, tanh_y, along_right, along_up, conic


def iota(shape, dim, kind=i32):
    return lax.broadcasted_iota(i32, shape, dim).astype(kind)


def one_hot(keys, out_ref):
    which = iota((256, 128), 0)
    for i in range(64):
        hot = jnp.broadcast_to(keys[i : i + 1, :], (256, 128)) == which
        at = 128 * (i % 16)
        out_ref[i // 16, :, at : at + 128] = jnp.where(hot, 1.0, 0.0).astype(bf16)


def project_kernel(
    params_ref, table_ref, out_ref, held_ref, hot_ref, rows_ref, found_ref, packed_ref, sem
):
    copy = pltpu.make_async_copy(params_ref, held_ref, sem)
    copy.start()
    slots = table_ref[...]
    high = lax.shift_right_logical(slots, 8)
    one_hot(slots & 255, hot_ref)
    row = iota((16, 59), 0)
    offset = iota((16, 59), 1) - row
    table = jnp.zeros((16, 59), f32)
    for view in range(VIEWS):
        weights = harmonics(*camera(view)[2])
        part = jnp.zeros((16, 59), f32)
        for k in range(16):
            part = jnp.where(offset == 11 + 3 * (k - view), weights[k], part)
        table = jnp.where((row >= 3 * view) & (row < 3 * view + 3), part, table)
    copy.wait()

    lead = held_ref[0:16, :].reshape(16, 16, 256)
    rows = [lead[i] for i in range(11)]
    colors = jnp.dot(
        table, held_ref[...], precision=HIGHEST, preferred_element_type=f32
    )
    colors = 0.5 + colors.reshape(16, 16, 256)
    _, _, _, scaled = geometry(rows)
    opacity = 1.0 / (1.0 + jnp.exp(-rows[10]))
    packed_ref[576:640, :] = jnp.zeros((64, 128), f32)
    which16 = iota((16, 128), 0)
    for view in range(VIEWS):
        tanh_x, tanh_y, _, _, conic = view_geometry(rows, scaled, view)
        projected = [8.0 + 6.0 * tanh_x, 8.0 + 6.0 * tanh_y, *conic, opacity]
        projected += [colors[3 * view + channel] for channel in range(3)]
        for half in range(2):
            lanes = slice(128 * half, 128 * half + 128)
            for f in range(8):
                rows_ref[half, pl.ds(f, 16, stride=8), :] = projected[f][:, lanes]
            rows_ref[half, 128:144, :] = projected[8][:, lanes]
        found_ref[...] = jnp.dot(
            jnp.concatenate([rows_ref[0], rows_ref[1]], axis=1).astype(bf16),
            hot_ref[view],
            preferred_element_type=f32,
        )
        for k in range(CAPV):
            lanes = slice(128 * k, 128 * k + 128)
            block = high[view * CAPV + k : view * CAPV + k + 1, :]
            block8 = jnp.broadcast_to(block, (8, 128))
            taken = found_ref[0:8, lanes]
            for h in range(1, 16):
                taken = jnp.where(block8 == h, found_ref[8 * h : 8 * h + 8, lanes], taken)
            group = 2 * view + k % 2
            at = 64 * group + 8 * (k // 2)
            packed_ref[at : at + 8, :] = taken
            here = jnp.broadcast_to(block, (16, 128)) == which16
            last = jnp.where(here, found_ref[128:144, lanes], 0.0)
            at = 512 + 8 * group + k // 2
            packed_ref[at : at + 1, :] = jnp.sum(last, axis=0, keepdims=True)
    out_ref[:, 0, :] = packed_ref[...].T


def window_mean(fields, window):
    count = len(fields)
    means = jnp.dot(
        jnp.concatenate(fields, axis=0), window, precision=HIGHEST, preferred_element_type=f32
    )
    return [means[192 * n : 192 * n + 192] for n in range(count)]


def window_mean_split(fields, window):
    field = jnp.concatenate(fields, axis=0)
    coarse, weight = field.astype(bf16), window.astype(bf16)
    fine = (field - coarse.astype(f32)).astype(bf16)
    weight_fine = (window - weight.astype(f32)).astype(bf16)
    means = jnp.dot(
        jnp.concatenate([coarse, fine, coarse], axis=1),
        jnp.concatenate([weight, weight, weight_fine], axis=0),
        preferred_element_type=f32,
    )
    return [means[192 * n : 192 * n + 192] for n in range(len(fields))]


def render_kernel(
    rows_ref,
    lists_ref,
    length_ref,
    target_hbm,
    window_hbm,
    out_ref,
    target_ref,
    window_ref,
    hot_ref,
    table_ref,
    slots_ref,
    first_ref,
    ninth_ref,
    entry_ref,
    column_ref,
    cover_ref,
    weight_ref,
    image_ref,
    partial_ref,
    moment_ref,
    spread_ref,
    total_ref,
    sems,
):
    pairs = (
        (target_hbm, target_ref),
        (window_hbm, window_ref),
    )
    later_copies = [
        pltpu.make_async_copy(source, target, sems.at[n])
        for n, (source, target) in enumerate(pairs)
    ]
    for copy in later_copies:
        copy.start()
    lists = lists_ref[...]
    one_hot((lists & 1) * 128 + lax.shift_right_logical(lists, 6), hot_ref)
    slot = lists & 63
    strays = jnp.where(lax.shift_right_logical(slot, 4) != iota((64, 128), 0) // 16, 1, 0)
    regular = jnp.max(strays) == 0
    which8 = iota((8, 128), 0)

    slots_ref[...] = rows_ref[:, 0, :].T
    first_ref[...] = jnp.zeros((512, 128), f32)
    ninth_ref[...] = jnp.zeros((64, 128), f32)
    for view in range(VIEWS):
        at, at9 = 128 * view, 512 + 16 * view
        table_ref[view] = jnp.concatenate(
            [
                jnp.concatenate([slots_ref[at : at + 64], slots_ref[at + 64 : at + 128]], axis=1),
                jnp.concatenate([slots_ref[at9 : at9 + 8], slots_ref[at9 + 8 : at9 + 16]], axis=1),
                jnp.zeros((8, 256), f32),
            ],
            axis=0,
        ).astype(bf16)
    for b in range(VIEWS):
        first = jnp.where(regular, b, 0)
        last = jnp.where(regular, b + 1, VIEWS)

        def fetch(view, carry, b=b):
            found = jnp.dot(table_ref[view], hot_ref[b], preferred_element_type=f32)
            for t in range(16):
                tile = b * 16 + t
                lanes = slice(128 * t, 128 * t + 128)
                pair = lax.shift_right_logical(lists_ref[tile : tile + 1, :] & 63, 1)
                pair = jnp.broadcast_to(pair, (8, 128)) - view * 8
                taken = first_ref[8 * tile : 8 * tile + 8, :]
                for k in range(8):
                    taken = jnp.where(pair == k, found[8 * k : 8 * k + 8, lanes], taken)
                first_ref[8 * tile : 8 * tile + 8, :] = taken
                ninth = jnp.where(pair == which8, found[64:72, lanes], 0.0)
                ninth_ref[tile : tile + 1, :] += jnp.sum(ninth, axis=0, keepdims=True)
            return carry

        lax.fori_loop(first, last, fetch, 0)

    length = jnp.concatenate([length_ref[...], length_ref[...]], axis=1)
    live = iota((128, 128), 0) < length
    for f in range(ROWS):
        own = first_ref[pl.ds(f, 64, stride=8), :] if f < 8 else ninth_ref[...]
        both = jnp.concatenate([own, own], axis=0).T
        column_ref[f] = both
        if f == 5:
            column_ref[ROWS] = jnp.where(live, both, 0.0)

    lane = iota((8, 128), 1)
    base_y = jnp.where(lane < 64, 0.5, 8.5)

    def entry_row(f, j):
        return jnp.broadcast_to(column_ref[f, pl.ds(j, 1), :], (8, 128))

    for half in range(2):
        place_x = iota((8, 128), 0, f32) + (8.0 * half + 0.5)

        def forward(j, carry, half=half, place_x=place_x):
            clear, image = carry
            clear, image = list(clear), [list(c) for c in image]
            dx = place_x - entry_row(0, j)
            dy = base_y - entry_row(1, j)
            conic0 = entry_row(2, j) * (-0.5 * log2e)
            conic1 = entry_row(3, j) * (-log2e)
            conic2 = entry_row(4, j) * (-0.5 * log2e)
            opacity = entry_row(ROWS, j)
            color = [entry_row(6 + c, j) for c in range(3)]
            cross = conic1 * dx
            exponent = conic0 * dx * dx + dy * (cross + conic2 * dy)
            slope = cross + conic2 * (2.0 * dy + 1.0)
            bend = 2.0 * conic2
            for y in range(8):
                coverage = opacity * jnp.exp2(exponent)
                weight = clear[y] * coverage
                clear[y] = clear[y] - weight
                for c in range(3):
                    image[c][y] = image[c][y] + weight * color[c]
                cover_ref[j, 2 * y + half] = coverage
                weight_ref[j, 2 * y + half] = weight
                if y < 7:
                    exponent = exponent + slope
                    slope = slope + bend
            return clear, image

        zero = jnp.zeros((8, 128), f32)
        start = ([jnp.ones((8, 128), f32)] * 8, [[zero] * 8] * 3)
        _, image = lax.fori_loop(0, 128, forward, start, unroll=8)
        for c in range(3):
            for y in range(8):
                image_ref[c, 16 * y + 8 * half : 16 * y + 8 * half + 8, :] = image[c][y]

    for copy in later_copies:
        copy.wait()
    shown = []
    for c in range(3):
        turned = image_ref[c].T
        shown.append(jnp.concatenate([turned[0:64], turned[64:128]], axis=1))
    shown = jnp.concatenate(shown, axis=0)
    goal = target_ref[...].reshape(192, 256)
    fields = [shown, shown * shown, shown * goal, goal, goal * goal]
    mean_x, square_x, product, mean_y, square_y = window_mean(fields, window_ref[...])
    var_x = square_x - mean_x * mean_x
    var_y = square_y - mean_y * mean_y
    covariance = product - mean_x * mean_y
    top_one = 2.0 * mean_x * mean_y + stabilizer_one
    top_two = 2.0 * covariance + stabilizer_two
    under_one = 1.0 / (mean_x * mean_x + mean_y * mean_y + stabilizer_one)
    under_two = 1.0 / (var_x + var_y + stabilizer_two)
    under = under_one * under_two
    similarity = top_one * top_two * under
    difference = shown - goal
    pixel_loss = (1.0 - loss_blend) * jnp.abs(difference) + loss_blend * (1.0 - similarity)
    loss = jnp.sum(pixel_loss)
    by_product = 2.0 * top_one * under
    by_square = -similarity * under_two
    by_mean = (
        2.0 * mean_y * top_two * under
        - 2.0 * mean_x * similarity * under_one
        - mean_y * by_product
        - 2.0 * mean_x * by_square
    )
    fields = [by_mean, by_square, by_product]
    by_mean, by_square, by_product = window_mean_split(fields, window_ref[...])
    slope = (1.0 - loss_blend) * jnp.where(
        difference > 0.0, 1.0, jnp.where(difference < 0.0, -1.0, 0.0)
    ) - loss_blend * (by_mean + 2.0 * shown * by_square + goal * by_product)
    for c in range(3):
        own = slope[64 * c : 64 * c + 64]
        image_ref[c] = jnp.concatenate([own[:, 0:128], own[:, 128:256]], axis=0).T

    for half in range(2):
        place_x = iota((8, 128), 0, f32) + (8.0 * half - 7.5)
        slope = [
            [image_ref[c, 16 * y + 8 * half : 16 * y + 8 * half + 8, :] for y in range(8)]
            for c in range(3)
        ]

        def backward(i, behind, half=half, place_x=place_x, slope=slope):
            j = 127 - i
            behind = list(behind)
            color = [entry_row(6 + c, j) for c in range(3)]
            by_color = [None] * 3
            sum0 = sum1 = sum2 = None
            for y in range(7, -1, -1):
                coverage = cover_ref[j, 2 * y + half]
                weight = weight_ref[j, 2 * y + half]
                own = slope[0][y] * color[0] + slope[1][y] * color[1] + slope[2][y] * color[2]
                excess = own - behind[y]
                behind[y] = behind[y] + coverage * excess
                push = weight * excess
                for c in range(3):
                    term = weight * slope[c][y]
                    by_color[c] = term if by_color[c] is None else by_color[c] + term
                sum0 = push if sum0 is None else sum0 + push
                if y > 0:
                    sum1 = sum0 if sum1 is None else sum1 + sum0
                    sum2 = sum1 if sum2 is None else sum2 + sum1
            along = sum0 * place_x
            parts = [sum0, along, along * place_x, sum1, sum1 * place_x, sum2, *by_color]
            if half == 0:
                for n in range(ROWS):
                    partial_ref[n, j] = parts[n]
            else:
                for n in range(ROWS):
                    whole = jnp.sum(parts[n] + partial_ref[n, j], axis=0, keepdims=True)
                    moment_ref[n, pl.ds(j, 1), :] = whole
            return behind

        lax.fori_loop(0, 128, backward, [jnp.zeros((8, 128), f32)] * 8, unroll=8)

    at_x = 8.0 - column_ref[0]
    at_y = jnp.where(iota((128, 128), 1) < 64, 0.5, 8.5) - column_ref[1]
    m, mx, mxx = moment_ref[0], moment_ref[1], moment_ref[2]
    my, mxy = moment_ref[3], moment_ref[4]
    myy = 2.0 * moment_ref[5] - my
    about_x = mx + at_x * m
    about_y = my + at_y * m
    about_xx = mxx + at_x * (mx + about_x)
    about_yy = myy + at_y * (my + about_y)
    about_xy = mxy + at_y * mx + at_x * about_y
    conic0, conic1, conic2 = column_ref[2], column_ref[3], column_ref[4]
    grads = [
        conic0 * about_x + conic1 * about_y,
        conic2 * about_y + conic1 * about_x,
        -0.5 * about_xx,
        -about_xy,
        -0.5 * about_yy,
        m / column_ref[5],
        moment_ref[6],
        moment_ref[7],
        moment_ref[8],
    ]
    for f in range(ROWS):
        both = grads[f].T
        whole = both[0:64] + both[64:128]
        coarse = whole.astype(bf16).astype(f32)
        entry_ref[f] = coarse
        moment_ref[f, 0:64, :] = whole - coarse

    nothing = jnp.zeros((8, 128), f32)
    for view in range(VIEWS):
        first = jnp.where(regular, view, 0)
        last = jnp.where(regular, view + 1, VIEWS)
        total_ref[...] = jnp.zeros((160, 256), f32)

        def block(b, carry, view=view):
            for t in range(16):
                tile = b * 16 + t
                here = lists_ref[pl.ds(tile, 1), :]
                pair = lax.shift_right_logical(here & 63, 1)
                hit = jnp.broadcast_to(pair, (8, 128)) == which8 + view * 8
                lanes = slice(128 * t, 128 * t + 128)
                for part, source in enumerate((entry_ref, moment_ref)):
                    pieces = []
                    for f in range(ROWS):
                        row = jnp.broadcast_to(source[f, pl.ds(tile, 1), :], (8, 128))
                        pieces.append(jnp.where(hit, row, 0.0))
                    pieces.append(nothing)
                    spread_ref[80 * part : 80 * part + 80, lanes] = jnp.concatenate(
                        pieces, axis=0
                    ).astype(bf16)
            total_ref[...] += lax.dot_general(
                spread_ref[...],
                hot_ref[b],
                (((1,), (1,)), ((), ())),
                preferred_element_type=f32,
            )
            return carry

        lax.fori_loop(first, last, block, 0)
        total = total_ref[0:80, :] + total_ref[80:160, :]
        for parity in range(2):
            at = 160 * view + 80 * parity
            slots_ref[at : at + 72, :] = total[0:72, 128 * parity : 128 * parity + 128]
            slots_ref[at + 72 : at + 80, :] = jnp.full((8, 128), loss, f32)
    out_ref[:, 0, :] = slots_ref[...].T


FACTORS = 11 * VIEWS + 9


def factors(params_ref, factor_ref):
    lead = params_ref[0:16, :].reshape(16, 16, 256)
    rows = [lead[i] for i in range(11)]
    extent, norm, unit, scaled = geometry(rows)
    opacity = 1.0 / (1.0 + jnp.exp(-rows[10]))
    for view in range(VIEWS):
        tanh_x, tanh_y, along_right, along_up, conic = view_geometry(rows, scaled, view)
        parts = [6.0 * (1.0 - tanh_x * tanh_x), 6.0 * (1.0 - tanh_y * tanh_y)]
        parts += [*along_right, *along_up, *conic]
        for n, part in enumerate(parts):
            factor_ref[11 * view + n] = part
    parts = [*unit, 1.0 / norm, *(focal_length * e for e in extent), opacity * (1.0 - opacity)]
    for n, part in enumerate(parts):
        factor_ref[11 * VIEWS + n] = part


def update_kernel(
    pixels,
    grads_ref,
    table_ref,
    spread_table_ref,
    params_hbm,
    first_hbm,
    second_hbm,
    new_params_ref,
    new_first_ref,
    new_second_ref,
    loss_ref,
    hot_ref,
    factor_ref,
    params_ref,
    first_ref,
    second_ref,
    coarse_ref,
    fine_ref,
    spread_ref,
    stack_ref,
    gradient_ref,
    result_ref,
    in_sems,
    sems,
):
    pairs = (
        (params_hbm, params_ref),
        (first_hbm, first_ref),
        (second_hbm, second_ref),
    )
    adam_copies = [
        pltpu.make_async_copy(source, target, in_sems.at[n])
        for n, (source, target) in enumerate(pairs)
    ]
    for copy in adam_copies:
        copy.start()
    one_hot(table_ref[...] & 255, hot_ref)
    adam_copies[0].wait()
    factors(params_ref, factor_ref)
    packed = grads_ref[:, 0, :].T
    loss_ref[...] = jnp.sum(packed[72:73, :], axis=1, keepdims=True) * (1.0 / pixels)
    coarse = packed.astype(bf16).astype(f32)
    coarse_ref[...] = coarse
    fine_ref[...] = packed - coarse
    high = lax.shift_right_logical(table_ref[...], 8)
    which16 = iota((16, 128), 0)

    zero = jnp.zeros((16, 256), f32)
    by_position = [zero] * 3
    by_extent = [zero] * 3
    by_rotation = [[zero] * 3 for _ in range(3)]
    by_opacity = zero
    by_color = []
    for view in range(VIEWS):
        for k in range(CAPV):
            slot = view * CAPV + k
            lanes = slice(128 * k, 128 * k + 128)
            hit = jnp.broadcast_to(high[slot : slot + 1, :], (16, 128)) == which16
            base = 160 * view + 80 * (k % 2) + k // 2
            for part, source in enumerate((coarse_ref, fine_ref)):
                for f in range(ROWS):
                    row = source[base + 8 * f : base + 8 * f + 1, :]
                    row = jnp.broadcast_to(row, (16, 128))
                    at = 144 * part + 16 * f
                    spread_ref[at : at + 16, lanes] = jnp.where(hit, row, 0.0).astype(bf16)
        total = lax.dot_general(
            spread_ref[...],
            hot_ref[view],
            (((1,), (1,)), ((), ())),
            preferred_element_type=f32,
        )
        total = total[0:144] + total[144:288]
        grads = [total[16 * f : 16 * f + 16] for f in range(ROWS)]

        right, upward, _ = camera(view)
        factor = [factor_ref[11 * view + n] for n in range(11)]
        along_right, along_up, (c0, c1, c2) = factor[2:5], factor[5:8], factor[8:11]
        by_x = grads[0] * factor[0]
        by_y = grads[1] * factor[1]
        g0, g1, g2 = grads[2:5]
        by_xx = -(g0 * c0 * c0 + g1 * c0 * c1 + g2 * c1 * c1)
        by_xy = -(2.0 * g0 * c0 * c1 + g1 * (c0 * c2 + c1 * c1) + 2.0 * g2 * c1 * c2)
        by_yy = -(g0 * c1 * c1 + g1 * c1 * c2 + g2 * c2 * c2)
        for i in range(3):
            if right[i] != 0.0:
                by_position[i] = by_position[i] + by_x * right[i]
            by_position[i] = by_position[i] + by_y * upward[i]
        for k in range(3):
            by_right = 2.0 * by_xx * along_right[k] + by_xy * along_up[k]
            by_up = 2.0 * by_yy * along_up[k] + by_xy * along_right[k]
            by_extent[k] = by_extent[k] + by_right * along_right[k] + by_up * along_up[k]
            for i in range(3):
                if right[i] != 0.0:
                    by_rotation[i][k] = by_rotation[i][k] + by_right * right[i]
                by_rotation[i][k] = by_rotation[i][k] + by_up * upward[i]
        by_opacity = by_opacity + grads[5]
        by_color += grads[6:9]

    w, x, y, z, by_norm, *scale, by_sigmoid = [factor_ref[11 * VIEWS + n] for n in range(9)]
    r = [[by_rotation[i][k] * scale[k] for k in range(3)] for i in range(3)]
    by_unit = [
        2.0 * (z * (r[1][0] - r[0][1]) + y * (r[0][2] - r[2][0]) + x * (r[2][1] - r[1][2])),
        2.0
        * (
            y * (r[0][1] + r[1][0])
            + z * (r[0][2] + r[2][0])
            + w * (r[2][1] - r[1][2])
            - 2.0 * x * (r[1][1] + r[2][2])
        ),
        2.0
        * (
            x * (r[0][1] + r[1][0])
            + z * (r[1][2] + r[2][1])
            + w * (r[0][2] - r[2][0])
            - 2.0 * y * (r[0][0] + r[2][2])
        ),
        2.0
        * (
            x * (r[0][2] + r[2][0])
            + y * (r[1][2] + r[2][1])
            + w * (r[1][0] - r[0][1])
            - 2.0 * z * (r[0][0] + r[1][1])
        ),
    ]
    unit = (w, x, y, z)
    along = sum(unit[i] * by_unit[i] for i in range(4))
    by_quaternion = [(by_unit[i] - unit[i] * along) * by_norm for i in range(4)]
    by_logit = by_opacity * by_sigmoid
    pieces = by_color + [zero] * 4 + by_position + by_extent + by_quaternion + [by_logit]
    pieces += [zero] * 5
    for n, piece in enumerate(pieces):
        stack_ref[n : n + 1, :] = piece.reshape(1, 4096)

    high, middle, low = (part.astype(bf16) for part in split(stack_ref[...]))
    gradient_ref[...] = jnp.dot(
        spread_table_ref[...],
        jnp.concatenate([high, middle, low, high, middle, high], axis=0),
        preferred_element_type=f32,
    )
    for copy in adam_copies[1:]:
        copy.wait()
    copies = []
    outs = (new_params_ref, new_first_ref, new_second_ref)
    for n, (start, stop) in enumerate(CHUNKS):
        at = slice(start, stop)
        gradient = gradient_ref[at, :]
        new_first = beta_first * first_ref[at, :] + (1.0 - beta_first) * gradient
        new_second = beta_second * second_ref[at, :] + (1.0 - beta_second) * gradient * gradient
        corrected_first = new_first * (1.0 / (1.0 - beta_first**adam_step))
        corrected_second = new_second * (1.0 / (1.0 - beta_second**adam_step))
        new_params = params_ref[at, :] - learning_rate * corrected_first / (
            jnp.sqrt(corrected_second) + adam_epsilon
        )
        for which, value in enumerate((new_params, new_first, new_second)):
            result_ref[which, at, :] = value
            copies.append(
                pltpu.make_async_copy(
                    result_ref.at[which, at, :], outs[which].at[at, :], sems.at[which, n]
                )
            )
            copies[-1].start()
    for copy in copies:
        copy.wait()


CHUNKS = ((0, 16), (16, 32), (32, 48), (48, 59))


def shards(params, first_moment, second_moment, send_table, tile_lists, list_length, target):
    devices = lax.axis_size("dev")
    table = jnp.swapaxes(send_table, 1, 2).reshape(64, 128)
    payload = jax.ShapeDtypeStruct((128, 1, PAYLOAD), f32)
    window = jnp.asarray(window_matrix())
    vmem = pl.BlockSpec(memory_space=pltpu.VMEM)
    anywhere = pl.BlockSpec(memory_space=pl.ANY)
    sent = pl.pallas_call(
        project_kernel,
        out_shape=payload,
        in_specs=[anywhere, vmem],
        scratch_shapes=[
            pltpu.VMEM((59, 4096), f32),
            pltpu.VMEM((4, 256, 2048), bf16),
            pltpu.VMEM((2, 144, 128), f32),
            pltpu.VMEM((144, 2048), f32),
            pltpu.VMEM((PAYLOAD, 128), f32),
            pltpu.SemaphoreType.DMA,
        ],
        compiler_params=pltpu.CompilerParams(vmem_limit_bytes=VMEM_BYTES),
        name="project",
    )(params, table)
    arrived = lax.all_to_all(sent, "dev", split_axis=0, concat_axis=0, tiled=True)
    slopes = pl.pallas_call(
        render_kernel,
        out_shape=payload,
        in_specs=[vmem] * 3 + [anywhere] * 2,
        scratch_shapes=[
            pltpu.VMEM((3, 64, 256), f32),
            pltpu.VMEM((256, 256), f32),
            pltpu.VMEM((4, 256, 2048), bf16),
            pltpu.VMEM((4, 80, 256), bf16),
            pltpu.VMEM((PAYLOAD, 128), f32),
            pltpu.VMEM((512, 128), f32),
            pltpu.VMEM((64, 128), f32),
            pltpu.VMEM((ROWS, 64, 128), f32),
            pltpu.VMEM((ROWS + 1, 128, 128), f32),
            pltpu.VMEM((128, 16, 8, 128), f32),
            pltpu.VMEM((128, 16, 8, 128), f32),
            pltpu.VMEM((3, 128, 128), f32),
            pltpu.VMEM((ROWS, 128, 8, 128), f32),
            pltpu.VMEM((ROWS, 128, 128), f32),
            pltpu.VMEM((160, 2048), bf16),
            pltpu.VMEM((160, 256), f32),
            pltpu.SemaphoreType.DMA((2,)),
        ],
        compiler_params=pltpu.CompilerParams(vmem_limit_bytes=VMEM_BYTES),
        name="render",
    )(
        arrived,
        tile_lists,
        list_length.reshape(1, 64),
        target,
        window,
    )
    returned = lax.all_to_all(slopes, "dev", split_axis=0, concat_axis=0, tiled=True)
    whole = jax.ShapeDtypeStruct(params.shape, f32)
    new_params, new_first, new_second, mean_loss = pl.pallas_call(
        functools.partial(update_kernel, 3.0 * target.shape[1] * 256 * devices),
        out_shape=(whole, whole, whole, jax.ShapeDtypeStruct((1, 1), f32)),
        in_specs=[vmem] * 3 + [anywhere] * 3,
        out_specs=(anywhere, anywhere, anywhere, vmem),
        scratch_shapes=[
            pltpu.VMEM((4, 256, 2048), bf16),
            pltpu.VMEM((FACTORS, 16, 256), f32),
            pltpu.VMEM((59, 4096), f32),
            pltpu.VMEM((59, 4096), f32),
            pltpu.VMEM((59, 4096), f32),
            pltpu.VMEM((PAYLOAD, 128), f32),
            pltpu.VMEM((PAYLOAD, 128), f32),
            pltpu.VMEM((288, 2048), bf16),
            pltpu.VMEM((32, 4096), f32),
            pltpu.VMEM((64, 4096), f32),
            pltpu.VMEM((3, 59, 4096), f32),
            pltpu.SemaphoreType.DMA((3,)),
            pltpu.SemaphoreType.DMA((3, len(CHUNKS))),
        ],
        compiler_params=pltpu.CompilerParams(vmem_limit_bytes=VMEM_BYTES),
        name="update",
    )(
        returned,
        table,
        jnp.asarray(spread_table()),
        params,
        first_moment,
        second_moment,
    )
    return new_params, new_first, new_second, mean_loss.reshape(())


def solution(mesh):
    placed = (
        P(None, "dev"),
        P(None, "dev"),
        P(None, "dev"),
        P("dev", None, None),
        P("dev", None),
        P("dev"),
        P(None, "dev", None),
    )
    return jax.shard_map(
        shards,
        mesh=mesh,
        in_specs=placed,
        out_specs=(P(None, "dev"), P(None, "dev"), P(None, "dev"), P()),
        check_vma=False,
    )
```
